256 devices in a mesh: dp: 8 (over x, core), tensor: 32 (over y, z).
Axes of the slice: x: 4, y: 4, z: 8, core: 2. Of those that a mesh axis runs over, the one named last changes fastest.
Arguments:
- tokens: bfloat16 [4096, 4096], P(('dp', 'tensor')), may hold values from -6 to 6
- cotangent: bfloat16 [4096, 4096], P(('dp', 'tensor')), may hold values from -12 to 12
- loss_mask: int32 [4096], P(('dp', 'tensor')), may hold values from 0 to 1, as said below
- gate_weight: bfloat16 [4096, 14336], P(None, 'tensor'), may hold values from -0.09375 to 0.09375
- up_weight: bfloat16 [4096, 14336], P(None, 'tensor'), may hold values from -0.09375 to 0.09375
- down_weight: bfloat16 [14336, 4096], P('tensor'), may hold values from -0.046875 to 0.046875
- probe_seed: int32 [1], replicated, may hold values from 0 to 1048575
Outputs:
- diag_gate: float32 [4096, 14336], P('dp', 'tensor')
The draws below stay inside these ranges and needn't reach their ends.
Inputs may be any that keep to these rules, and one draw needn't show every extreme that they name: `loss_mask`: 0 or 1; the first entry is 1.
All inputs are finite; a program needn't handle non-finite values.
Results may differ from the reference program's by a relative error of at most 0.0029.
Values may be sent and summed in bfloat16 or wider, within the bound.
A program may use at most 128 MiB of HBM per device.

```python
import jax
import jax.numpy as jnp
from jax import lax

D = 4096
FF = 14336
TOK_REP = 512
TOKENS = 4096
N_DP = 8


def draw_loss_mask(key, part):
    key = jax.random.fold_in(key, 7)
    position = jnp.arange(TOKENS, dtype=jnp.int32)
    threshold = 64 + 128 * position // TOKENS
    ticket = jax.random.randint(key, (TOKENS,), 0, 256, dtype=jnp.int32)
    live_flags = jnp.where(ticket < threshold, 1, 0).astype(jnp.int32)
    return jnp.where(position == 0, 1, live_flags).astype(jnp.int32)


def steps_of(stream_key, extent, cuts, low, high):
    factor_of = 1.0
    for axis_at, shards_of in cuts:
        heights = jax.random.uniform(jax.random.fold_in(jax.random.fold_in(stream_key, 6), axis_at), (shards_of,), jnp.float32, low / len(cuts), high / len(cuts))
        factor_of = factor_of * jnp.repeat(jnp.exp(heights), extent[axis_at] // shards_of).reshape((-1,) + (1,) * (len(extent) - 1 - axis_at))
    return factor_of


def centred(rng, dims, width, reach, shards=(), kind=jnp.bfloat16):
    result = width * jax.random.normal(rng, dims, jnp.float32)
    if shards:
        result = result * steps_of(rng, dims, shards, -0.22, 0.18)
    return jnp.clip(result, -reach, reach).astype(kind)


def setup_inputs(seed: int = 0) -> dict:
    key_of = jax.random.split(jax.random.key(seed), 8)
    tokens = centred(key_of[0], (TOKENS, D), 1.0, 6.0, ((0, 256),))
    cotangent = centred(key_of[1], (TOKENS, D), 3.0, 12.0, ((0, 256),))
    loss_mask = draw_loss_mask(jax.random.fold_in(key_of[7], 71), 0)
    gate_weight = centred(key_of[3], (D, FF), D ** -0.5, 0.09375, ((1, 32),))
    up_weight = centred(key_of[4], (D, FF), D ** -0.5, 0.09375, ((1, 32),))
    down_weight = centred(key_of[5], (FF, D), FF ** -0.5, 0.046875, ((0, 32),))
    probe_seed = jax.random.randint(key_of[6], (1,), 0, 1048576).astype(jnp.int32)
    return {"tokens": tokens, "cotangent": cotangent, "loss_mask": loss_mask, "gate_weight": gate_weight, "up_weight": up_weight, "down_weight": down_weight, "probe_seed": probe_seed}


def probe_signs(seed_value, row_count, col_count, first_col, full_width):
    row_index = lax.broadcasted_iota(jnp.int32, (row_count, col_count), 0)
    col_index = lax.broadcasted_iota(jnp.int32, (row_count, col_count), 1) + first_col
    hashed = (row_index * full_width + col_index) * jnp.int32(-1640531535) + seed_value * jnp.int32(668265263)
    hashed = hashed ^ lax.shift_right_logical(hashed, jnp.full_like(hashed, 15))
    hashed = hashed * jnp.int32(739982445)
    hashed = hashed ^ lax.shift_right_logical(hashed, jnp.full_like(hashed, 12))
    hashed = hashed * jnp.int32(695872825)
    hashed = hashed ^ lax.shift_right_logical(hashed, jnp.full_like(hashed, 15))
    lowbit = lax.shift_right_logical(hashed, jnp.full_like(hashed, 16)) & jnp.int32(1)
    return jnp.int32(1) - jnp.int32(2) * lowbit


def curvature(gate_pre):
    sigmoid_val = jax.nn.sigmoid(gate_pre)
    return sigmoid_val * (1.0 - sigmoid_val) * (2.0 + gate_pre * (1.0 - 2.0 * sigmoid_val))


def reference(tokens, cotangent, loss_mask, gate_weight, up_weight, down_weight, probe_seed):
    sign_table = probe_signs(probe_seed[0], D, FF, jnp.int32(0), FF)
    probe_bf = sign_table.astype(jnp.bfloat16)
    live_flags = loss_mask.astype(jnp.float32)
    live_count = jnp.sum(live_flags)
    masked = (cotangent.astype(jnp.float32) * live_flags[:, None]).astype(jnp.bfloat16)
    token_blocks = tokens.reshape(N_DP, TOK_REP, D)
    masked_blocks = masked.reshape(N_DP, TOK_REP, D)

    def replica_step(running, block_pair):
        features, masked_rows = block_pair
        gate_pre = jnp.dot(features, gate_weight, preferred_element_type=jnp.float32)
        up_proj = jnp.dot(features, up_weight, preferred_element_type=jnp.float32)
        tangent = jnp.dot(features, probe_bf, preferred_element_type=jnp.float32)
        back_grad = jnp.dot(masked_rows, down_weight.T, preferred_element_type=jnp.float32)
        operand = (back_grad * up_proj * curvature(gate_pre) * tangent).astype(jnp.bfloat16)
        return running + jnp.dot(features.T, operand, preferred_element_type=jnp.float32), None

    total_sum, unused = lax.scan(replica_step, jnp.zeros((D, FF), jnp.float32), (token_blocks, masked_blocks))
    hessian = total_sum / live_count
    return sign_table.astype(jnp.float32) * hessian
```

```python
import jax
import jax.numpy as jnp
from jax import lax
from jax.experimental import pallas as pl
from jax.experimental.pallas import tpu as pltpu
from jax.sharding import PartitionSpec as P

FF = 14336
D = 4096
NY, NZ, NX = 4, 8, 4
ROWS = 16
WIDTH = 448
CHUNK = 128
N_CHUNK = 4
OUT_ROWS = 512
HALF = WIDTH // 2
MASK_AT = 2 * D
WIDE = 2 * D + 128
FAM = ((0, 3328), (3328, WIDE - 3328))
DZ = (0, 1, -1, 2, -2, 3, -3, 4)
DY = (0, 1, -1, 2)
MESH = pl.DeviceIdType.MESH
NT = (((1,), (1,)), ((), ()))
TN = (((0,), (0,)), ((), ()))
F32 = jnp.float32
BF16 = jnp.bfloat16


def slot(dy, dz):
    return DZ.index(dz) * 4 + DY.index(dy)


def arrival_order():
    order = [(-1, 0, 0), (1, 0, 0), (0, -1, 0), (0, 1, 0), (0, -1, 1), (0, 1, 1), (-1, 0, 1), (1, 0, 1), (2, 0, 0)]
    for s in (1, 2, 3):
        order += [(-1, -s, 0), (-1, s, 0), (1, -s, 0), (1, s, 0), (-1, -s, 1), (1, -s, 1)]
        order += [(0, -s - 1, 0), (0, s + 1, 0)] if s < 3 else [(0, 4, 0)]
        order += [(-1, s, 1), (1, s, 1)]
        if s == 1:
            order += [(2, 0, 1)]
        order += [(0, -s - 1, 1), (0, s + 1, 1)] if s < 3 else [(0, 4, 1)]
        order += [(2, -s, 1), (2, -s, 0), (2, s, 0), (2, s, 1)]
    order += [(-1, 4, 0), (1, 4, 0), (-1, 4, 1), (1, 4, 1), (2, 4, 0), (2, 4, 1)]
    return order


def curvature(gate_pre):
    sigmoid_val = jax.nn.sigmoid(gate_pre)
    return sigmoid_val * (1.0 - sigmoid_val) * (2.0 + gate_pre * (1.0 - 2.0 * sigmoid_val))


def kernel(
    tok_ref, cot_ref, mask_ref, seed_ref, wg_hbm, wu_hbm, wd_hbm, out_ref,
    x, cot, wg, wu, wd, sign, gate, up, tan, op, own, core_out, core_in, x_out, x_in, cnt_out, cnt_in,
    local_sem, ag_send, ag_recv, core_send, core_recv, x_send, x_recv, cnt_send, cnt_recv,
):
    dp = lax.axis_index("dp")
    me = lax.axis_index("tensor")
    core = lax.rem(dp, 2)
    xi = lax.div(dp, 2)
    yi = lax.div(me, NZ)
    zi = lax.rem(me, NZ)

    def at_y(step):
        return dp, lax.rem(yi + step + NY, NY) * NZ + zi

    def at_z(step):
        return dp, yi * NZ + lax.rem(zi + step + NZ, NZ)

    def at_x(step):
        return lax.rem(xi + step + NX, NX) * 2 + core, me

    partner = (xi * 2 + 1 - core, me)
    away = 1 - 2 * core

    tok_copy = pltpu.make_async_copy(tok_ref, x.at[pl.ds(0, ROWS), pl.ds(0, D)], local_sem.at[0])
    cot_copy = pltpu.make_async_copy(cot_ref, cot, local_sem.at[1])
    wg_copy = pltpu.make_async_copy(wg_hbm, wg, local_sem.at[2])
    wu_copy = pltpu.make_async_copy(wu_hbm, wu, local_sem.at[3])
    wd_copy = pltpu.make_async_copy(wd_hbm, wd, local_sem.at[4])
    tok_copy.start()
    cot_copy.start()

    peers = [at_y(1), at_y(-1), at_z(1), at_z(-1), partner, at_x(1), at_x(-1), at_x(2)]
    barrier = pltpu.get_barrier_semaphore()
    for peer in peers:
        pl.semaphore_signal(barrier, inc=1, device_id=peer, device_id_type=MESH)

    row = lax.broadcasted_iota(jnp.int32, (ROWS, 128), 0)
    live = jnp.zeros((ROWS, 128), F32)
    for r in range(ROWS):
        live = jnp.where(row == r, mask_ref[r].astype(F32), live)
    x[0:ROWS, MASK_AT:WIDE] = live.astype(BF16)
    cot_copy.wait()
    x[0:ROWS, D:MASK_AT] = (cot[...].astype(F32) * live[:, 0:1]).astype(BF16)
    tok_copy.wait()
    pl.semaphore_wait(barrier, len(peers))

    def block(at, fam):
        start, size = FAM[fam]
        if not isinstance(at, int):
            return x.at[pl.ds(pl.multiple_of(at * ROWS, ROWS), ROWS), pl.ds(start, size)]
        return x.at[pl.ds(at * ROWS, ROWS), pl.ds(start, size)]

    def hop(fam, src, dst, device):
        return pltpu.make_async_remote_copy(
            src_ref=block(src, fam),
            dst_ref=block(dst, fam),
            send_sem=ag_send.at[fam, dst],
            recv_sem=ag_recv.at[fam, dst],
            device_id=device,
            device_id_type=MESH,
        )

    def z_sends(dy, dz, fam):
        if dz <= 0 and dz > -3:
            hop(fam, slot(dy, dz), slot(dy, dz - 1), at_z(1)).start()
        if dz >= 0 and dz < 3:
            hop(fam, slot(dy, dz), slot(dy, dz + 1), at_z(-1)).start()
        if dz == 3:
            hop(fam, DZ.index(-3) * 4 + DY.index(dy) - 4 * core, slot(dy, 4), at_z(away)).start()

    def y_sends(dy, dz, fam):
        if dy == 0:
            hop(fam, slot(0, dz), slot(-1, dz), at_y(1)).start()
            hop(fam, slot(0, dz), slot(1, dz), at_y(-1)).start()
        if dy == 1:
            hop(fam, DZ.index(dz) * 4 + 2 - core, slot(2, dz), at_y(away)).start()

    y_sends(0, 0, 0)
    z_sends(0, 0, 0)
    z_sends(0, 0, 1)
    y_sends(0, 0, 1)
    wg_copy.start()
    wu_copy.start()
    wd_copy.start()

    first_col = me * WIDTH
    col_term = (lax.broadcasted_iota(jnp.int32, (1, WIDTH), 1) + first_col) * jnp.int32(-1640531535)
    col_term = col_term + seed_ref[0] * jnp.int32(668265263)

    def make_signs(k):
        def run():
            size = D // 16
            i = lax.broadcasted_iota(jnp.int32, (size, 1), 0) + k * size
            h = (i * FF) * jnp.int32(-1640531535) + col_term
            h = h ^ lax.shift_right_logical(h, jnp.full_like(h, 15))
            h = h * jnp.int32(739982445)
            h = h ^ lax.shift_right_logical(h, jnp.full_like(h, 12))
            h = h * jnp.int32(695872825)
            h = h ^ lax.shift_left(h, jnp.full_like(h, 15))
            sign[k * size : (k + 1) * size, :] = jnp.where(h < 0, F32(-1.0), F32(1.0)).astype(BF16)

        return run

    def tokens_of(c):
        return slice(c * CHUNK, (c + 1) * CHUNK)

    def make_gate(c):
        def run():
            if c == 0:
                wg_copy.wait()
            gate[...] = jnp.dot(x[tokens_of(c), 0:D], wg[...], preferred_element_type=F32)

        return run

    def make_up(c):
        def run():
            if c == 0:
                wu_copy.wait()
            up[...] = jnp.dot(x[tokens_of(c), 0:D], wu[...], preferred_element_type=F32)

        return run

    def make_tan(c):
        def run():
            tan[...] = jnp.dot(x[tokens_of(c), 0:D], sign[...], preferred_element_type=F32)

        return run

    def make_op(c):
        def run():
            if c == 0:
                wd_copy.wait()
            back = lax.dot_general(x[tokens_of(c), D:MASK_AT], wd[...], NT, preferred_element_type=F32)
            operand = back * up[...] * curvature(gate[...]) * tan[...]
            op[tokens_of(c), :] = operand.astype(BF16)

        return run

    order = arrival_order()
    here = {(0, 0, 0), (0, 0, 1)}
    work = [(None, make_signs(k)) for k in range(16)]
    for c in range(N_CHUNK):
        needs = {(dy, dz, fam) for dz in DZ[2 * c : 2 * c + 2] for dy in DY for fam in (0, 1)}
        work += [(needs, make_gate(c)), (needs, make_up(c)), (needs, make_tan(c)), (needs, make_op(c))]
    for dy, dz, fam in order:
        hop(fam, 0, slot(dy, dz), partner).wait_recv()
        here.add((dy, dz, fam))
        if fam == 0:
            if dy == 1 and dz == 0:
                y_sends(1, 0, 0)
            z_sends(dy, dz, 0)
        else:
            if dy == 0:
                z_sends(0, dz, 1)
                y_sends(0, dz, 1)
            elif dy == 1:
                y_sends(1, dz, 1)
        if work and (work[0][0] is None or work[0][0] <= here):
            work.pop(0)[1]()
    for _, run in work:
        run()

    count = jnp.sum(x[:, MASK_AT:WIDE].astype(F32), axis=0, keepdims=True)
    cnt_out[0] = jnp.broadcast_to(count, (8, 128))

    def count_copy(src, dst, device):
        return pltpu.make_async_remote_copy(
            src_ref=cnt_out.at[src],
            dst_ref=cnt_in.at[dst],
            send_sem=cnt_send.at[dst],
            recv_sem=cnt_recv.at[dst],
            device_id=device,
            device_id_type=MESH,
        )

    count_copy(0, 0, partner).start()

    def core_copy(k):
        return pltpu.make_async_remote_copy(
            src_ref=core_out.at[k],
            dst_ref=core_in.at[k],
            send_sem=core_send.at[k],
            recv_sem=core_recv.at[k],
            device_id=partner,
            device_id_type=MESH,
        )

    def rows_of(half):
        return pl.ds(half * HALF, HALF)

    def x_copy(k, half, dst, device):
        return pltpu.make_async_remote_copy(
            src_ref=x_out.at[k - 1, rows_of(half)],
            dst_ref=x_in.at[dst, rows_of(half)],
            send_sem=x_send.at[k - 1, half],
            recv_sem=x_recv.at[dst, half],
            device_id=device,
            device_id_type=MESH,
        )

    def product(k, of_core):
        start = (lax.rem(xi + k, NX) * 2 + of_core) * OUT_ROWS
        cols = pl.ds(pl.multiple_of(start, OUT_ROWS), OUT_ROWS)
        return lax.dot_general(op[...], x[:, cols], TN, preferred_element_type=F32)

    for k in (2, 1, 3, 0):
        core_out[k] = product(k, 1 - core).astype(BF16)
        core_copy(k).start()
        own[k] = product(k, core)
        if k == 2:
            continue
        last = {1: 2, 3: 1, 0: 3}[k]
        core_copy(last).wait_recv()
        own[last] += core_in[last].astype(F32)
        if last == 2:
            x_out[1] = own[2].astype(BF16)
            x_copy(2, 0, 1, at_x(1)).start()
            x_copy(2, 1, 1, at_x(-1)).start()
        elif last == 1:
            x_out[0, HALF:WIDTH] = own[1, HALF:WIDTH].astype(BF16)
            x_copy(1, 1, 0, at_x(1)).start()
        elif last == 3:
            x_out[2, 0:HALF] = own[3, 0:HALF].astype(BF16)
            x_copy(3, 0, 2, at_x(-1)).start()
    count_copy(0, 0, partner).wait_recv()
    pair = cnt_out[0] + cnt_in[0]
    cnt_out[1] = pair
    count_copy(1, 1, at_x(1)).start()
    count_copy(1, 2, at_x(2)).start()
    count_copy(1, 3, at_x(-1)).start()
    core_copy(0).wait_recv()
    own[0] += core_in[0].astype(F32)

    x_copy(2, 0, 1, at_x(1)).wait_recv()
    x_out[0, 0:HALF] = (own[1, 0:HALF] + x_in[1, 0:HALF].astype(F32)).astype(BF16)
    x_copy(1, 0, 0, at_x(1)).start()
    x_copy(2, 1, 1, at_x(-1)).wait_recv()
    x_out[2, HALF:WIDTH] = (own[3, HALF:WIDTH] + x_in[1, HALF:WIDTH].astype(F32)).astype(BF16)
    x_copy(3, 1, 2, at_x(-1)).start()

    for d in (1, 2, 3):
        count_copy(1, d, at_x(1)).wait_recv()
    total = pair + cnt_in[1] + cnt_in[2] + cnt_in[3]
    live_count = total[0:1, 0:1]
    x_copy(1, 1, 0, at_x(1)).wait_recv()
    x_copy(3, 0, 2, at_x(-1)).wait_recv()
    x_copy(1, 0, 0, at_x(1)).wait_recv()
    x_copy(3, 1, 2, at_x(-1)).wait_recv()
    hess = own[0] + x_in[0].astype(F32) + x_in[2].astype(F32)
    own_signs = sign[pl.ds(pl.multiple_of(dp * OUT_ROWS, OUT_ROWS), OUT_ROWS), :].astype(F32)
    out_ref[...] = own_signs * (hess.T / live_count)

    for dy, dz, fam in order:
        hop(fam, 0, slot(dy, dz), partner).wait_send()
    for k in range(4):
        core_copy(k).wait_send()
    for k in (1, 2, 3):
        for half in (0, 1):
            x_copy(k, half, 0, at_x(1)).wait_send()
    for d in range(4):
        count_copy(0, d, at_x(1)).wait_send()


def per_device(tokens, cotangent, loss_mask, gate_weight, up_weight, down_weight, probe_seed):
    any_space = pl.BlockSpec(memory_space=pl.ANY)
    smem = pl.BlockSpec(memory_space=pltpu.SMEM)
    vmem = pltpu.VMEM
    dma = pltpu.SemaphoreType.DMA
    return pl.pallas_call(
        kernel,
        out_shape=jax.ShapeDtypeStruct((OUT_ROWS, WIDTH), F32),
        in_specs=[any_space, any_space, smem, smem, any_space, any_space, any_space],
        out_specs=pl.BlockSpec(memory_space=vmem),
        scratch_shapes=[
            vmem((NY * NZ * ROWS, WIDE), BF16),
            vmem((ROWS, D), BF16),
            vmem((D, WIDTH), BF16),
            vmem((D, WIDTH), BF16),
            vmem((WIDTH, D), BF16),
            vmem((D, WIDTH), BF16),
            vmem((CHUNK, WIDTH), F32),
            vmem((CHUNK, WIDTH), F32),
            vmem((CHUNK, WIDTH), F32),
            vmem((N_CHUNK * CHUNK, WIDTH), BF16),
            vmem((4, WIDTH, OUT_ROWS), F32),
            vmem((4, WIDTH, OUT_ROWS), BF16),
            vmem((4, WIDTH, OUT_ROWS), BF16),
            vmem((3, WIDTH, OUT_ROWS), BF16),
            vmem((3, WIDTH, OUT_ROWS), BF16),
            vmem((2, 8, 128), F32),
            vmem((4, 8, 128), F32),
            dma((5,)),
            dma((2, NY * NZ)),
            dma((2, NY * NZ)),
            dma((4,)),
            dma((4,)),
            dma((3, 2)),
            dma((3, 2)),
            dma((4,)),
            dma((4,)),
        ],
        compiler_params=pltpu.CompilerParams(
            collective_id=0, has_side_effects=True, vmem_limit_bytes=56 * 2**20
        ),
        cost_estimate=pl.CostEstimate(flops=9_400_000_000, bytes_accessed=12_000_000, transcendentals=230_000),
    )(tokens, cotangent, loss_mask, probe_seed, gate_weight, up_weight, down_weight)


def solution(mesh):
    in_specs = (
        P(("dp", "tensor"), None),
        P(("dp", "tensor"), None),
        P(("dp", "tensor")),
        P(None, "tensor"),
        P(None, "tensor"),
        P("tensor", None),
        P(),
    )
    return jax.shard_map(
        per_device, mesh=mesh, in_specs=in_specs, out_specs=P("dp", "tensor"), check_vma=False
    )
```

```python
import jax
import jax.numpy as jnp
from jax import lax
from jax.experimental import pallas as pl
from jax.experimental.pallas import tpu as pltpu
from jax.sharding import PartitionSpec as P

FF = 14336
D = 4096
NY, NZ, NX = 4, 8, 4
ROWS = 16
WIDTH = 448
CHUNK = 128
N_CHUNK = 4
OUT_ROWS = 512
HALF = WIDTH // 2
MASK_AT = 2 * D
WIDE = 2 * D + 128
SPLIT = 24 * 128
FAM = ((0, SPLIT), (SPLIT, WIDE - SPLIT))
DZ = (0, 1, -1, 2, -2, 3, -3, 4)
DY = (0, 1, -1, 2)
MESH = pl.DeviceIdType.MESH
NT = (((1,), (1,)), ((), ()))
TN = (((0,), (0,)), ((), ()))
F32 = jnp.float32
BF16 = jnp.bfloat16


def slot(dy, dz):
    return DZ.index(dz) * 4 + DY.index(dy)


PLAN = (
    (2, 0, 0, 0), (2, 1, 0, 0), (1, -1, 0, 0), (1, 0, -1, 0), (1, 1, 0, 0), (2, 2, 0, 0), (1, 0, -1, 1),
    (1, -1, 0, 1), (2, 3, 0, 0), (2, 4, 0, 0), (1, 0, 1, 1), (2, 5, 0, 0), (2, 6, 0, 0), (2, 7, 0, 0),
    (1, 1, 0, 1), (1, 0, 1, 0), (0, -1, 0, 0), (1, 2, 0, 0), (0, 0, -1, 1), (1, 0, -2, 1), (0, -1, 0, 1),
    (1, 2, 0, 1), (1, -1, -1, 1), (0, 0, 1, 1), (1, 0, 2, 1), (1, -1, -1, 0), (1, 1, -1, 1), (0, 0, -2, 1),
    (1, 0, -3, 1), (1, -1, 1, 1), (0, 0, 2, 1), (1, 0, 3, 1), (1, 1, 1, 1), (1, -1, 1, 0), (0, -1, -1, 1),
    (1, 2, -1, 1), (0, 0, -3, 1), (1, 0, 4, 1), (0, -1, 1, 1), (1, 2, 1, 1), (0, 1, 0, 0), (1, 1, -1, 0),
    (1, 1, 1, 0), (1, -1, -2, 1), (0, 2, 0, 0), (1, 2, -1, 0), (1, 1, -2, 1), (1, 2, 1, 0), (0, 0, -1, 0),
    (1, 0, -2, 0), (1, -1, 2, 1), (0, 0, 1, 0), (1, 0, 2, 0), (0, -1, -1, 0), (1, -1, -2, 0), (1, 1, 2, 1),
    (0, -1, 1, 0), (1, -1, 2, 0), (0, -1, -2, 1), (1, 2, -2, 1), (0, 1, -1, 0), (1, 1, -2, 0), (0, 1, 0, 1),
    (0, 2, 0, 1), (0, 1, 1, 1), (0, 2, 1, 1), (0, 1, 1, 0), (0, 2, 1, 0), (2, 8, 0, 0), (1, 1, 2, 0),
    (2, 9, 0, 0), (0, -1, 2, 1), (1, 2, 2, 1), (0, 2, -1, 0), (1, 2, -2, 0), (2, 10, 0, 0), (1, -1, -3, 1),
    (1, 2, 2, 0), (2, 11, 0, 0), (0, 0, -2, 0), (1, 0, -3, 0), (1, 1, -3, 1), (0, 0, 2, 0), (1, 0, 3, 0),
    (0, -1, -2, 0), (1, -1, -3, 0), (0, 0, 3, 1), (1, -1, 3, 1), (0, -1, 2, 0), (1, -1, 3, 0), (1, 1, 3, 1),
    (0, 1, -2, 0), (1, 1, -3, 0), (0, 1, -1, 1), (0, 2, -1, 1), (0, 1, 2, 1), (0, 1, 2, 0), (0, 2, 2, 1),
    (0, 2, 2, 0), (2, 12, 0, 0), (1, 1, 3, 0), (0, -1, -3, 1), (1, 2, -3, 1), (2, 13, 0, 0), (0, 2, -2, 0),
    (1, 2, -3, 0), (2, 14, 0, 0), (1, 2, 3, 0), (0, -1, 3, 1), (1, 2, 3, 1), (2, 15, 0, 0), (0, 0, -3, 0),
    (1, 0, 4, 0), (0, 0, 4, 1), (1, -1, 4, 1), (0, -1, -3, 0), (1, -1, 4, 0), (0, 1, -3, 0), (1, 1, 4, 0),
    (1, 1, 4, 1), (0, 2, -3, 0), (1, 2, 4, 0), (0, 1, -2, 1), (0, 2, -2, 1), (0, 0, 3, 0), (0, -1, 3, 0),
    (0, 1, 3, 1), (0, 1, 3, 0), (0, 2, 3, 0), (0, 2, 3, 1), (2, 16, 0, 0), (2, 17, 0, 0), (0, -1, 4, 1),
    (1, 2, 4, 1), (2, 18, 0, 0), (2, 19, 0, 0), (0, 0, 4, 0), (0, -1, 4, 0), (0, 1, 4, 0), (0, 2, 4, 0),
    (2, 20, 0, 0), (2, 21, 0, 0), (2, 22, 0, 0), (0, 1, -3, 1), (0, 2, -3, 1), (0, 1, 4, 1), (0, 2, 4, 1),
    (2, 23, 0, 0), (2, 24, 0, 0), (2, 25, 0, 0), (2, 26, 0, 0),
)


def curvature(gate_pre):
    sigmoid_val = jax.nn.sigmoid(gate_pre)
    return sigmoid_val * (1.0 - sigmoid_val) * (2.0 + gate_pre * (1.0 - 2.0 * sigmoid_val))


def kernel(
    tok_ref, cot_ref, mask_ref, seed_ref, wg_hbm, wu_hbm, wd_hbm, out_ref,
    x, cot, wg, wu, wd, sign, gate, up, tan, op, own, core_out, core_in, x_out, x_in, cnt_out, cnt_in,
    local_sem, ag_send, ag_recv, core_send, core_recv, x_send, x_recv, cnt_send, cnt_recv,
):
    dp = lax.axis_index("dp")
    me = lax.axis_index("tensor")
    core = lax.rem(dp, 2)
    xi = lax.div(dp, 2)
    yi = lax.div(me, NZ)
    zi = lax.rem(me, NZ)

    away = 1 - 2 * core

    def at_y(step):
        return dp, lax.rem(yi + away * step + NY, NY) * NZ + zi

    def at_z(step):
        return dp, yi * NZ + lax.rem(zi + away * step + NZ, NZ)

    def at_x(step):
        return lax.rem(xi + step + NX, NX) * 2 + core, me

    partner = (xi * 2 + 1 - core, me)

    tok_copy = pltpu.make_async_copy(tok_ref, x.at[pl.ds(0, ROWS), pl.ds(0, D)], local_sem.at[0])
    cot_copy = pltpu.make_async_copy(cot_ref, cot, local_sem.at[1])
    wg_copy = pltpu.make_async_copy(wg_hbm, wg, local_sem.at[2])
    wu_copy = pltpu.make_async_copy(wu_hbm, wu, local_sem.at[3])
    wd_copy = pltpu.make_async_copy(wd_hbm, wd, local_sem.at[4])
    tok_copy.start()
    cot_copy.start()

    peers = [at_y(1), at_y(-1), at_z(1), at_z(-1), partner, at_x(1), at_x(-1), at_x(2)]
    barrier = pltpu.get_barrier_semaphore()
    for peer in peers:
        pl.semaphore_signal(barrier, inc=1, device_id=peer, device_id_type=MESH)

    row = lax.broadcasted_iota(jnp.int32, (ROWS, 128), 0)
    live = jnp.zeros((ROWS, 128), F32)
    for r in range(ROWS):
        live = jnp.where(row == r, mask_ref[r].astype(F32), live)
    x[0:ROWS, MASK_AT:WIDE] = live.astype(BF16)
    cot_copy.wait()
    x[0:ROWS, D:MASK_AT] = (cot[...].astype(F32) * live[:, 0:1]).astype(BF16)
    tok_copy.wait()
    pl.semaphore_wait(barrier, len(peers))

    def block(at, fam):
        start, size = FAM[fam]
        return x.at[pl.ds(at * ROWS, ROWS), pl.ds(start, size)]

    def hop(dy, dz, fam):
        if dy != 0 and (fam == 1 or dz == 0):
            came_dy, came_dz, device = (0, dz, at_y(-dy)) if dy != 2 else (-1, dz, at_y(1))
        else:
            came_dy, came_dz, device = (dy, dz - 1, at_z(-1)) if 0 < dz < 4 else (dy, (dz + 1 if dz < 0 else -3), at_z(1))
        dst = slot(dy, dz)
        return pltpu.make_async_remote_copy(
            src_ref=block(slot(came_dy, came_dz), fam),
            dst_ref=block(dst, fam),
            send_sem=ag_send.at[fam, dst],
            recv_sem=ag_recv.at[fam, dst],
            device_id=device,
            device_id_type=MESH,
        )

    wg_copy.start()
    wu_copy.start()
    wd_copy.start()
    first_col = me * WIDTH
    col_term = (lax.broadcasted_iota(jnp.int32, (WIDTH, 1), 0) + first_col) * jnp.int32(-1640531535)
    col_term = col_term + seed_ref[0] * jnp.int32(668265263)

    def make_signs(k):
        def run():
            size = D // 8
            i = lax.broadcasted_iota(jnp.int32, (1, size), 1) + k * size
            h = (i * FF) * jnp.int32(-1640531535) + col_term
            h = h ^ lax.shift_right_logical(h, jnp.full_like(h, 15))
            h = h * jnp.int32(739982445)
            h = h ^ lax.shift_right_logical(h, jnp.full_like(h, 12))
            h = h * jnp.int32(695872825)
            h = h ^ lax.shift_left(h, jnp.full_like(h, 15))
            sign[:, k * size : (k + 1) * size] = jnp.where(h < 0, F32(-1.0), F32(1.0)).astype(BF16)

        return run

    def tokens_of(c):
        return slice(c * CHUNK, (c + 1) * CHUNK)

    def make_dot(c, out, w, copy, cols):
        def run():
            if copy is not None:
                copy.wait()
            part = lax.dot_general(x[tokens_of(c), cols], w[:, cols], NT, preferred_element_type=F32)
            if cols.start == 0:
                out[...] = part
            else:
                out[...] += part

        return run

    def make_op(c):
        def run():
            if c == 0:
                wd_copy.wait()
            back = lax.dot_general(x[tokens_of(c), D:MASK_AT], wd[...], NT, preferred_element_type=F32)
            operand = back * up[...] * curvature(gate[...]) * tan[...]
            op[tokens_of(c), :] = operand.astype(BF16)

        return run

    work = [make_signs(k) for k in range(8)]
    for c in range(N_CHUNK):
        for cols in (slice(0, D),) if c < N_CHUNK - 1 else (slice(0, SPLIT), slice(SPLIT, D)):
            work.append(make_dot(c, gate, wg, wg_copy if c == 0 else None, cols))
            work.append(make_dot(c, up, wu, wu_copy if c == 0 else None, cols))
            work.append(make_dot(c, tan, sign, None, cols))
        work.append(make_op(c))
    for what, dy, dz, fam in PLAN:
        if what == 0:
            hop(dy, dz, fam).wait_recv()
        elif what == 1:
            hop(dy, dz, fam).start()
        else:
            work[dy]()

    count = jnp.sum(x[:, MASK_AT:WIDE].astype(F32), axis=0, keepdims=True)
    cnt_out[0] = jnp.broadcast_to(count, (8, 128))

    def count_copy(src, dst, device):
        return pltpu.make_async_remote_copy(
            src_ref=cnt_out.at[src],
            dst_ref=cnt_in.at[dst],
            send_sem=cnt_send.at[dst],
            recv_sem=cnt_recv.at[dst],
            device_id=device,
            device_id_type=MESH,
        )

    count_copy(0, 0, partner).start()

    def core_copy(k):
        return pltpu.make_async_remote_copy(
            src_ref=core_out.at[k],
            dst_ref=core_in.at[k],
            send_sem=core_send.at[k],
            recv_sem=core_recv.at[k],
            device_id=partner,
            device_id_type=MESH,
        )

    def rows_of(half):
        return pl.ds(half * HALF, HALF)

    def x_copy(k, half, dst, device):
        return pltpu.make_async_remote_copy(
            src_ref=x_out.at[k - 1, rows_of(half)],
            dst_ref=x_in.at[dst, rows_of(half)],
            send_sem=x_send.at[k - 1, half],
            recv_sem=x_recv.at[dst, half],
            device_id=device,
            device_id_type=MESH,
        )

    def product(k, of_core):
        start = (lax.rem(xi + k, NX) * 2 + of_core) * OUT_ROWS
        cols = pl.ds(pl.multiple_of(start, OUT_ROWS), OUT_ROWS)
        return lax.dot_general(op[...], x[:, cols], TN, preferred_element_type=F32)

    for k in (2, 1, 3, 0):
        core_out[k] = product(k, 1 - core).astype(BF16)
        core_copy(k).start()
        own[k] = product(k, core)
        if k == 2:
            continue
        last = {1: 2, 3: 1, 0: 3}[k]
        core_copy(last).wait_recv()
        own[last] += core_in[last].astype(F32)
        if last == 2:
            x_out[1] = own[2].astype(BF16)
            x_copy(2, 0, 1, at_x(1)).start()
            x_copy(2, 1, 1, at_x(-1)).start()
        elif last == 1:
            x_out[0, HALF:WIDTH] = own[1, HALF:WIDTH].astype(BF16)
            x_copy(1, 1, 0, at_x(1)).start()
        elif last == 3:
            x_out[2, 0:HALF] = own[3, 0:HALF].astype(BF16)
            x_copy(3, 0, 2, at_x(-1)).start()
    count_copy(0, 0, partner).wait_recv()
    pair = cnt_out[0] + cnt_in[0]
    cnt_out[1] = pair
    count_copy(1, 1, at_x(1)).start()
    count_copy(1, 2, at_x(2)).start()
    count_copy(1, 3, at_x(-1)).start()
    core_copy(0).wait_recv()
    own[0] += core_in[0].astype(F32)

    x_copy(2, 0, 1, at_x(1)).wait_recv()
    x_out[0, 0:HALF] = (own[1, 0:HALF] + x_in[1, 0:HALF].astype(F32)).astype(BF16)
    x_copy(1, 0, 0, at_x(1)).start()
    x_copy(2, 1, 1, at_x(-1)).wait_recv()
    x_out[2, HALF:WIDTH] = (own[3, HALF:WIDTH] + x_in[1, HALF:WIDTH].astype(F32)).astype(BF16)
    x_copy(3, 1, 2, at_x(-1)).start()

    for d in (1, 2, 3):
        count_copy(1, d, at_x(1)).wait_recv()
    total = pair + cnt_in[1] + cnt_in[2] + cnt_in[3]
    live_count = total[0:1, 0:1]
    x_copy(1, 1, 0, at_x(1)).wait_recv()
    x_copy(3, 0, 2, at_x(-1)).wait_recv()
    x_copy(1, 0, 0, at_x(1)).wait_recv()
    x_copy(3, 1, 2, at_x(-1)).wait_recv()
    hess = own[0] + x_in[0].astype(F32) + x_in[2].astype(F32)
    own_signs = sign[:, pl.ds(pl.multiple_of(dp * OUT_ROWS, OUT_ROWS), OUT_ROWS)].astype(F32)
    out_ref[...] = own_signs * (hess / live_count)

    for what, dy, dz, fam in PLAN:
        if what == 1:
            hop(dy, dz, fam).wait_send()
    for k in range(4):
        core_copy(k).wait_send()
    for k in (1, 2, 3):
        for half in (0, 1):
            x_copy(k, half, 0, at_x(1)).wait_send()
    for d in range(4):
        count_copy(0, d, at_x(1)).wait_send()


def per_device(tokens, cotangent, loss_mask, gate_weight, up_weight, down_weight, probe_seed):
    any_space = pl.BlockSpec(memory_space=pl.ANY)
    smem = pl.BlockSpec(memory_space=pltpu.SMEM)
    vmem = pltpu.VMEM
    dma = pltpu.SemaphoreType.DMA
    out = pl.pallas_call(
        kernel,
        out_shape=jax.ShapeDtypeStruct((WIDTH, OUT_ROWS), F32),
        in_specs=[any_space, any_space, smem, smem, any_space, any_space, any_space],
        out_specs=pl.BlockSpec(memory_space=vmem),
        scratch_shapes=[
            vmem((NY * NZ * ROWS, WIDE), BF16),
            vmem((ROWS, D), BF16),
            vmem((WIDTH, D), BF16),
            vmem((WIDTH, D), BF16),
            vmem((WIDTH, D), BF16),
            vmem((WIDTH, D), BF16),
            vmem((CHUNK, WIDTH), F32),
            vmem((CHUNK, WIDTH), F32),
            vmem((CHUNK, WIDTH), F32),
            vmem((N_CHUNK * CHUNK, WIDTH), BF16),
            vmem((4, WIDTH, OUT_ROWS), F32),
            vmem((4, WIDTH, OUT_ROWS), BF16),
            vmem((4, WIDTH, OUT_ROWS), BF16),
            vmem((3, WIDTH, OUT_ROWS), BF16),
            vmem((3, WIDTH, OUT_ROWS), BF16),
            vmem((2, 8, 128), F32),
            vmem((4, 8, 128), F32),
            dma((5,)),
            dma((2, NY * NZ)),
            dma((2, NY * NZ)),
            dma((4,)),
            dma((4,)),
            dma((3, 2)),
            dma((3, 2)),
            dma((4,)),
            dma((4,)),
        ],
        compiler_params=pltpu.CompilerParams(
            collective_id=0, has_side_effects=True, vmem_limit_bytes=56 * 2**20
        ),
        cost_estimate=pl.CostEstimate(flops=9_400_000_000, bytes_accessed=12_000_000, transcendentals=230_000),
    )(tokens, cotangent, loss_mask, probe_seed, gate_weight.T, up_weight.T, down_weight)
    return out.T


def solution(mesh):
    in_specs = (
        P(("dp", "tensor"), None),
        P(("dp", "tensor"), None),
        P(("dp", "tensor")),
        P(None, "tensor"),
        P(None, "tensor"),
        P("tensor", None),
        P(),
    )
    return jax.shard_map(
        per_device, mesh=mesh, in_specs=in_specs, out_specs=P("dp", "tensor"), check_vma=False
    )
```

```python
import jax
import jax.numpy as jnp
from jax import lax
from jax.experimental import pallas as pl
from jax.experimental.pallas import tpu as pltpu
from jax.sharding import PartitionSpec as P

FF = 14336
D = 4096
NY, NZ, NX = 4, 8, 4
ROWS = 16
WIDTH = 448
CHUNK = 256
N_CHUNK = 2
OUT_ROWS = 512
HALF = WIDTH // 2
MASK_AT = 2 * D
WIDE = 2 * D + 128
SPLIT = 25 * 128
FAM = ((0, SPLIT), (SPLIT, WIDE - SPLIT))
DZ = (0, 1, -1, 2, -2, 3, -3, 4)
DY = (0, 1, -1, 2)
MESH = pl.DeviceIdType.MESH
NT = (((1,), (1,)), ((), ()))
F32 = jnp.float32
BF16 = jnp.bfloat16


def slot(dy, dz):
    return DZ.index(dz) * 4 + DY.index(dy)


PLAN = (
    (2, 0, 0, 0), (2, 1, 0, 0), (2, 2, 0, 0), (2, 3, 0, 0), (2, 4, 0, 0), (2, 5, 0, 0), (2, 6, 0, 0),
    (2, 7, 0, 0), (0, -1, 0, 0), (1, 2, 0, 0), (0, 0, -1, 1), (1, 0, -2, 1), (1, -1, -1, 1), (1, 1, -1, 1),
    (1, -1, -1, 0), (1, -1, 1, 0), (0, 0, 1, 1), (1, 0, 2, 1), (1, -1, 1, 1), (0, 1, 0, 0), (1, 1, -1, 0),
    (1, 1, 1, 1), (1, 1, 1, 0), (0, 2, 0, 0), (1, 2, -1, 0), (0, -1, 0, 1), (1, 2, 0, 1), (1, 2, 1, 0),
    (0, 0, -2, 1), (1, 0, -3, 1), (1, -1, -2, 1), (0, 0, 2, 1), (1, 0, 3, 1), (1, 1, -2, 1), (0, 0, -1, 0),
    (1, 0, -2, 0), (1, -1, 2, 1), (0, 0, 1, 0), (1, 0, 2, 0), (1, 1, 2, 1), (0, -1, -1, 0), (1, -1, -2, 0),
    (0, -1, 1, 0), (1, -1, 2, 0), (0, -1, -1, 1), (1, 2, -1, 1), (0, 1, -1, 0), (1, 1, -2, 0), (0, 1, 1, 0),
    (1, 1, 2, 0), (0, -1, 1, 1), (1, 2, 1, 1), (0, 2, -1, 0), (1, 2, -2, 0), (0, 0, -3, 1), (1, -1, -3, 1),
    (0, 2, 1, 0), (1, 2, 2, 0), (1, 0, 4, 1), (1, 1, -3, 1), (0, 0, -2, 0), (1, 0, -3, 0), (0, 0, 3, 1),
    (1, -1, 3, 1), (0, 0, 2, 0), (1, 0, 3, 0), (0, -1, -2, 0), (1, -1, -3, 0), (1, 1, 3, 1), (0, -1, 2, 0),
    (1, -1, 3, 0), (0, -1, -2, 1), (1, 2, -2, 1), (0, 1, -2, 0), (1, 1, -3, 0), (0, 1, 2, 0), (0, 2, 2, 0),
    (2, 8, 0, 0), (2, 9, 0, 0), (1, 1, 3, 0), (0, -1, 2, 1), (1, 2, 2, 1), (2, 10, 0, 0), (0, 2, -2, 0),
    (1, 2, -3, 0), (0, 0, 4, 1), (1, -1, 4, 1), (1, 2, 3, 0), (0, 0, -3, 0), (1, 0, 4, 0), (1, 1, 4, 1),
    (0, -1, -3, 0), (1, -1, 4, 0), (0, -1, -3, 1), (1, 2, -3, 1), (0, 1, -3, 0), (1, 1, 4, 0), (0, -1, 3, 1),
    (1, 2, 3, 1), (0, 2, -3, 0), (1, 2, 4, 0), (0, 1, 0, 1), (0, 1, -1, 1), (0, 1, 1, 1), (0, 2, 0, 1),
    (0, 1, 2, 1), (0, 2, -1, 1), (0, 2, 1, 1), (0, 2, 2, 1), (2, 11, 0, 0), (2, 12, 0, 0), (2, 13, 0, 0),
    (2, 14, 0, 0), (0, -1, 4, 1), (1, 2, 4, 1), (0, 0, 3, 0), (0, -1, 3, 0), (0, 1, 3, 0), (0, 2, 3, 0),
    (0, 0, 4, 0), (0, -1, 4, 0), (0, 1, 4, 0), (0, 2, 4, 0), (2, 15, 0, 0), (2, 16, 0, 0), (2, 17, 0, 0),
    (0, 1, -2, 1), (0, 1, -3, 1), (0, 1, 3, 1), (0, 2, -2, 1), (0, 1, 4, 1), (0, 2, -3, 1), (0, 2, 3, 1),
    (0, 2, 4, 1), (2, 18, 0, 0), (2, 19, 0, 0), (2, 20, 0, 0), (2, 21, 0, 0),
)


def curvature(gate_pre):
    sigmoid_val = jax.nn.sigmoid(gate_pre)
    return sigmoid_val * (1.0 - sigmoid_val) * (2.0 + gate_pre * (1.0 - 2.0 * sigmoid_val))


def kernel(
    tok_ref, cot_ref, mask_ref, seed_ref, wg_hbm, wu_hbm, wd_hbm, out_ref,
    x, cot, wg, wu, wd, sign, gate, up, tan, op, own, core_out, core_in, x_out, x_in, cnt_out, cnt_in,
    local_sem, ag_send, ag_recv, core_send, core_recv, x_send, x_recv, cnt_send, cnt_recv,
):
    dp = lax.axis_index("dp")
    me = lax.axis_index("tensor")
    core = lax.rem(dp, 2)
    xi = lax.div(dp, 2)
    yi = lax.div(me, NZ)
    zi = lax.rem(me, NZ)

    away = 1 - 2 * core

    def at_y(step):
        return dp, lax.rem(yi + away * step + NY, NY) * NZ + zi

    def at_z(step):
        return dp, yi * NZ + lax.rem(zi + away * step + NZ, NZ)

    def at_x(step):
        return lax.rem(xi + step + NX, NX) * 2 + core, me

    partner = (xi * 2 + 1 - core, me)

    tok_copy = pltpu.make_async_copy(tok_ref, x.at[pl.ds(0, ROWS), pl.ds(0, D)], local_sem.at[0])
    cot_copy = pltpu.make_async_copy(cot_ref, cot, local_sem.at[1])
    wg_copy = pltpu.make_async_copy(wg_hbm, wg, local_sem.at[2])
    wu_copy = pltpu.make_async_copy(wu_hbm, wu, local_sem.at[3])
    wd_copy = pltpu.make_async_copy(wd_hbm, wd, local_sem.at[4])
    tok_copy.start()
    cot_copy.start()

    peers = [at_y(1), at_y(-1), at_z(1), at_z(-1), partner, at_x(1), at_x(-1), at_x(2)]
    barrier = pltpu.get_barrier_semaphore()
    for peer in peers:
        pl.semaphore_signal(barrier, inc=1, device_id=peer, device_id_type=MESH)

    tok_copy.wait()
    pl.semaphore_wait(barrier, len(peers))

    def block(at, fam):
        start, size = FAM[fam]
        return x.at[pl.ds(at * ROWS, ROWS), pl.ds(start, size)]

    def hop(dy, dz, fam):
        if dy != 0 and (fam == 1 or dz == 0):
            came_dy, came_dz, device = (0, dz, at_y(-dy)) if dy != 2 else (-1, dz, at_y(1))
        else:
            came_dy, came_dz, device = (dy, dz - 1, at_z(-1)) if 0 < dz < 4 else (dy, (dz + 1 if dz < 0 else -3), at_z(1))
        dst = slot(dy, dz)
        return pltpu.make_async_remote_copy(
            src_ref=block(slot(came_dy, came_dz), fam),
            dst_ref=block(dst, fam),
            send_sem=ag_send.at[fam, dst],
            recv_sem=ag_recv.at[fam, dst],
            device_id=device,
            device_id_type=MESH,
        )

    for dst in ((-1, 0, 0), (1, 0, 0), (0, -1, 0), (0, 1, 0)):
        hop(*dst).start()
    row = lax.broadcasted_iota(jnp.int32, (ROWS, 128), 0)
    live = jnp.zeros((ROWS, 128), F32)
    for r in range(ROWS):
        live = jnp.where(row == r, mask_ref[r].astype(F32), live)
    x[0:ROWS, MASK_AT:WIDE] = live.astype(BF16)
    cot_copy.wait()
    x[0:ROWS, D:MASK_AT] = (cot[...].astype(F32) * live[:, 0:1]).astype(BF16)
    for dst in ((0, -1, 1), (0, 1, 1), (-1, 0, 1), (1, 0, 1)):
        hop(*dst).start()

    wg_copy.start()
    wu_copy.start()
    wd_copy.start()
    first_col = me * WIDTH
    col_term = (lax.broadcasted_iota(jnp.int32, (WIDTH, 1), 0) + first_col) * jnp.int32(-1640531535)
    col_term = col_term + seed_ref[0] * jnp.int32(668265263)

    def make_signs(k):
        def run():
            size = D // 8
            i = lax.broadcasted_iota(jnp.int32, (1, size), 1) + k * size
            h = (i * FF) * jnp.int32(-1640531535) + col_term
            h = h ^ lax.shift_right_logical(h, jnp.full_like(h, 15))
            h = h * jnp.int32(739982445)
            h = h ^ lax.shift_right_logical(h, jnp.full_like(h, 12))
            h = h * jnp.int32(695872825)
            h = h ^ lax.shift_left(h, jnp.full_like(h, 15))
            sign[:, k * size : (k + 1) * size] = jnp.where(h < 0, F32(-1.0), F32(1.0)).astype(BF16)

        return run

    def tokens_of(c):
        return slice(c * CHUNK, (c + 1) * CHUNK)

    def make_dot(c, out, w, copy, cols):
        def run():
            if copy is not None:
                copy.wait()
            part = lax.dot_general(w[:, cols], x[tokens_of(c), cols], NT, preferred_element_type=F32)
            if cols.start == 0:
                out[...] = part
            else:
                out[...] += part

        return run

    def make_op(c):
        def run():
            if c == 0:
                wd_copy.wait()
            back = lax.dot_general(wd[...], x[tokens_of(c), D:MASK_AT], NT, preferred_element_type=F32)
            operand = back * up[...] * curvature(gate[...]) * tan[...]
            op[:, tokens_of(c)] = operand.astype(BF16)

        return run

    work = [make_signs(k) for k in range(8)]
    for c in range(N_CHUNK):
        for cols in (slice(0, SPLIT), slice(SPLIT, D)):
            work.append(make_dot(c, gate, wg, wg_copy if c == cols.start == 0 else None, cols))
            work.append(make_dot(c, up, wu, wu_copy if c == cols.start == 0 else None, cols))
            work.append(make_dot(c, tan, sign, None, cols))
        work.append(make_op(c))
    for what, dy, dz, fam in PLAN:
        if what == 0:
            hop(dy, dz, fam).wait_recv()
        elif what == 1:
            hop(dy, dz, fam).start()
        else:
            work[dy]()

    count = jnp.sum(x[:, MASK_AT:WIDE].astype(F32), axis=0, keepdims=True)
    cnt_out[0] = jnp.broadcast_to(count, (8, 128))

    def count_copy(src, dst, device):
        return pltpu.make_async_remote_copy(
            src_ref=cnt_out.at[src],
            dst_ref=cnt_in.at[dst],
            send_sem=cnt_send.at[dst],
            recv_sem=cnt_recv.at[dst],
            device_id=device,
            device_id_type=MESH,
        )

    count_copy(0, 0, partner).start()

    def core_copy(k):
        return pltpu.make_async_remote_copy(
            src_ref=core_out.at[k],
            dst_ref=core_in.at[k],
            send_sem=core_send.at[k],
            recv_sem=core_recv.at[k],
            device_id=partner,
            device_id_type=MESH,
        )

    def rows_of(half):
        return pl.ds(half * HALF, HALF)

    def x_copy(k, half, dst, device):
        return pltpu.make_async_remote_copy(
            src_ref=x_out.at[k - 1, rows_of(half)],
            dst_ref=x_in.at[dst, rows_of(half)],
            send_sem=x_send.at[k - 1, half],
            recv_sem=x_recv.at[dst, half],
            device_id=device,
            device_id_type=MESH,
        )

    def product(k, of_core):
        start = (lax.rem(xi + k, NX) * 2 + of_core) * OUT_ROWS
        cols = pl.ds(pl.multiple_of(start, OUT_ROWS), OUT_ROWS)
        return jnp.dot(op[...], x[:, cols], preferred_element_type=F32)

    for k in (2, 1, 3, 0):
        core_out[k] = product(k, 1 - core).astype(BF16)
        core_copy(k).start()
        own[k] = product(k, core)
        if k == 2:
            continue
        last = {1: 2, 3: 1, 0: 3}[k]
        core_copy(last).wait_recv()
        own[last] += core_in[last].astype(F32)
        if last == 2:
            x_out[1] = own[2].astype(BF16)
            x_copy(2, 0, 1, at_x(1)).start()
            x_copy(2, 1, 1, at_x(-1)).start()
        elif last == 1:
            x_out[0, HALF:WIDTH] = own[1, HALF:WIDTH].astype(BF16)
            x_copy(1, 1, 0, at_x(1)).start()
        elif last == 3:
            x_out[2, 0:HALF] = own[3, 0:HALF].astype(BF16)
            x_copy(3, 0, 2, at_x(-1)).start()
    count_copy(0, 0, partner).wait_recv()
    pair = cnt_out[0] + cnt_in[0]
    cnt_out[1] = pair
    count_copy(1, 1, at_x(1)).start()
    count_copy(1, 2, at_x(2)).start()
    count_copy(1, 3, at_x(-1)).start()
    core_copy(0).wait_recv()
    own[0] += core_in[0].astype(F32)

    x_copy(2, 0, 1, at_x(1)).wait_recv()
    x_out[0, 0:HALF] = (own[1, 0:HALF] + x_in[1, 0:HALF].astype(F32)).astype(BF16)
    x_copy(1, 0, 0, at_x(1)).start()
    x_copy(2, 1, 1, at_x(-1)).wait_recv()
    x_out[2, HALF:WIDTH] = (own[3, HALF:WIDTH] + x_in[1, HALF:WIDTH].astype(F32)).astype(BF16)
    x_copy(3, 1, 2, at_x(-1)).start()

    for d in (1, 2, 3):
        count_copy(1, d, at_x(1)).wait_recv()
    total = pair + cnt_in[1] + cnt_in[2] + cnt_in[3]
    live_count = total[0:1, 0:1]
    own_cols = pl.ds(pl.multiple_of(dp * OUT_ROWS, OUT_ROWS), OUT_ROWS)
    x_copy(1, 1, 0, at_x(1)).wait_recv()
    own[0, HALF:WIDTH] += x_in[0, HALF:WIDTH].astype(F32)
    x_copy(3, 0, 2, at_x(-1)).wait_recv()
    own[0, 0:HALF] += x_in[2, 0:HALF].astype(F32)
    x_copy(1, 0, 0, at_x(1)).wait_recv()
    hess = own[0, 0:HALF] + x_in[0, 0:HALF].astype(F32)
    out_ref[0:HALF, :] = sign[0:HALF, own_cols].astype(F32) * (hess / live_count)
    x_copy(3, 1, 2, at_x(-1)).wait_recv()
    hess = own[0, HALF:WIDTH] + x_in[2, HALF:WIDTH].astype(F32)
    out_ref[HALF:WIDTH, :] = sign[HALF:WIDTH, own_cols].astype(F32) * (hess / live_count)

    for at in range(1, NY * NZ):
        for fam in (0, 1):
            hop(DY[at % 4], DZ[at // 4], fam).wait_send()
    for k in range(4):
        core_copy(k).wait_send()
    for k in (1, 2, 3):
        for half in (0, 1):
            x_copy(k, half, 0, at_x(1)).wait_send()
    for d in range(4):
        count_copy(0, d, at_x(1)).wait_send()


def per_device(tokens, cotangent, loss_mask, gate_weight, up_weight, down_weight, probe_seed):
    any_space = pl.BlockSpec(memory_space=pl.ANY)
    smem = pl.BlockSpec(memory_space=pltpu.SMEM)
    vmem = pltpu.VMEM
    dma = pltpu.SemaphoreType.DMA
    out = pl.pallas_call(
        kernel,
        out_shape=jax.ShapeDtypeStruct((WIDTH, OUT_ROWS), F32),
        in_specs=[any_space, any_space, smem, smem, any_space, any_space, any_space],
        out_specs=pl.BlockSpec(memory_space=vmem),
        scratch_shapes=[
            vmem((NY * NZ * ROWS, WIDE), BF16),
            vmem((ROWS, D), BF16),
            vmem((WIDTH, D), BF16),
            vmem((WIDTH, D), BF16),
            vmem((WIDTH, D), BF16),
            vmem((WIDTH, D), BF16),
            vmem((WIDTH, CHUNK), F32),
            vmem((WIDTH, CHUNK), F32),
            vmem((WIDTH, CHUNK), F32),
            vmem((WIDTH, N_CHUNK * CHUNK), BF16),
            vmem((4, WIDTH, OUT_ROWS), F32),
            vmem((4, WIDTH, OUT_ROWS), BF16),
            vmem((4, WIDTH, OUT_ROWS), BF16),
            vmem((3, WIDTH, OUT_ROWS), BF16),
            vmem((3, WIDTH, OUT_ROWS), BF16),
            vmem((2, 8, 128), F32),
            vmem((4, 8, 128), F32),
            dma((5,)),
            dma((2, NY * NZ)),
            dma((2, NY * NZ)),
            dma((4,)),
            dma((4,)),
            dma((3, 2)),
            dma((3, 2)),
            dma((4,)),
            dma((4,)),
        ],
        compiler_params=pltpu.CompilerParams(
            collective_id=0, has_side_effects=True, vmem_limit_bytes=56 * 2**20
        ),
        cost_estimate=pl.CostEstimate(flops=9_400_000_000, bytes_accessed=12_000_000, transcendentals=230_000),
    )(tokens, cotangent, loss_mask, probe_seed, gate_weight.T, up_weight.T, down_weight)
    return out.T


def solution(mesh):
    in_specs = (
        P(("dp", "tensor"), None),
        P(("dp", "tensor"), None),
        P(("dp", "tensor")),
        P(None, "tensor"),
        P(None, "tensor"),
        P("tensor", None),
        P(),
    )
    return jax.shard_map(
        per_device, mesh=mesh, in_specs=in_specs, out_specs=P("dp", "tensor"), check_vma=False
    )
```

```python
import jax
import jax.numpy as jnp
from jax import lax
from jax.experimental import pallas as pl
from jax.experimental.pallas import tpu as pltpu
from jax.sharding import PartitionSpec as P

FF = 14336
D = 4096
NY, NZ, NX = 4, 8, 4
ROWS = 16
WIDTH = 448
CHUNK = 256
N_CHUNK = 2
OUT_ROWS = 512
HALF = WIDTH // 2
MASK_AT = 2 * D
WIDE = 2 * D + 128
SPLIT = 25 * 128
FAM = ((0, SPLIT), (SPLIT, WIDE - SPLIT))
DZ = (0, 1, -1, 2, -2, 3, -3, 4)
DY = (0, 1, -1, 2)
MESH = pl.DeviceIdType.MESH
NT = (((1,), (1,)), ((), ()))
F32 = jnp.float32
BF16 = jnp.bfloat16


def slot(dy, dz):
    return DZ.index(dz) * 4 + DY.index(dy)


PLAN = (
    (2, 0, 0, 0), (2, 1, 0, 0), (2, 2, 0, 0), (2, 3, 0, 0), (2, 4, 0, 0), (2, 5, 0, 0), (2, 6, 0, 0),
    (2, 7, 0, 0), (0, -1, 0, 0), (1, 2, 0, 0), (0, 0, -1, 1), (1, 0, -2, 1), (1, -1, -1, 1), (1, 1, -1, 1),
    (1, -1, -1, 0), (1, -1, 1, 0), (0, 0, 1, 1), (1, 0, 2, 1), (1, -1, 1, 1), (0, 1, 0, 0), (1, 1, -1, 0),
    (1, 1, 1, 1), (1, 1, 1, 0), (0, 2, 0, 0), (1, 2, -1, 0), (0, -1, 0, 1), (1, 2, 0, 1), (1, 2, 1, 0),
    (0, 0, -2, 1), (1, 0, -3, 1), (1, -1, -2, 1), (0, 0, 2, 1), (1, 0, 3, 1), (1, 1, -2, 1), (0, 0, -1, 0),
    (1, 0, -2, 0), (1, -1, 2, 1), (0, 0, 1, 0), (1, 0, 2, 0), (1, 1, 2, 1), (0, -1, -1, 0), (1, -1, -2, 0),
    (0, -1, 1, 0), (1, -1, 2, 0), (0, -1, -1, 1), (1, 2, -1, 1), (0, 1, -1, 0), (1, 1, -2, 0), (0, 1, 1, 0),
    (1, 1, 2, 0), (0, -1, 1, 1), (1, 2, 1, 1), (0, 2, -1, 0), (1, 2, -2, 0), (0, 0, -3, 1), (1, -1, -3, 1),
    (0, 2, 1, 0), (1, 2, 2, 0), (1, 0, 4, 1), (1, 1, -3, 1), (0, 0, -2, 0), (1, 0, -3, 0), (0, 0, 3, 1),
    (1, -1, 3, 1), (0, 0, 2, 0), (1, 0, 3, 0), (0, -1, -2, 0), (1, -1, -3, 0), (1, 1, 3, 1), (0, -1, 2, 0),
    (1, -1, 3, 0), (0, -1, -2, 1), (1, 2, -2, 1), (0, 1, -2, 0), (1, 1, -3, 0), (0, 1, 2, 0), (0, 2, 2, 0),
    (2, 8, 0, 0), (2, 9, 0, 0), (1, 1, 3, 0), (0, -1, 2, 1), (1, 2, 2, 1), (2, 10, 0, 0), (0, 2, -2, 0),
    (1, 2, -3, 0), (0, 0, 4, 1), (1, -1, 4, 1), (1, 2, 3, 0), (0, 0, -3, 0), (1, 0, 4, 0), (1, 1, 4, 1),
    (0, -1, -3, 0), (1, -1, 4, 0), (0, -1, -3, 1), (1, 2, -3, 1), (0, 1, -3, 0), (1, 1, 4, 0), (0, -1, 3, 1),
    (1, 2, 3, 1), (0, 2, -3, 0), (1, 2, 4, 0), (0, 1, 0, 1), (0, 1, -1, 1), (0, 1, 1, 1), (0, 2, 0, 1),
    (0, 1, 2, 1), (0, 2, -1, 1), (0, 2, 1, 1), (0, 2, 2, 1), (2, 11, 0, 0), (2, 12, 0, 0), (2, 13, 0, 0),
    (2, 14, 0, 0), (0, -1, 4, 1), (1, 2, 4, 1), (0, 0, 3, 0), (0, -1, 3, 0), (0, 1, 3, 0), (0, 2, 3, 0),
    (0, 0, 4, 0), (0, -1, 4, 0), (0, 1, 4, 0), (0, 2, 4, 0), (2, 15, 0, 0), (2, 16, 0, 0), (2, 17, 0, 0),
    (0, 1, -2, 1), (0, 1, -3, 1), (0, 1, 3, 1), (0, 2, -2, 1), (0, 1, 4, 1), (0, 2, -3, 1), (0, 2, 3, 1),
    (0, 2, 4, 1), (2, 18, 0, 0), (2, 19, 0, 0), (2, 20, 0, 0), (2, 21, 0, 0),
)


def curvature(gate_pre):
    sigmoid_val = jax.nn.sigmoid(gate_pre)
    return sigmoid_val * (1.0 - sigmoid_val) * (2.0 + gate_pre * (1.0 - 2.0 * sigmoid_val))


def kernel(
    tok_ref, cot_ref, mask_ref, seed_ref, wg_hbm, wu_hbm, wd_hbm, out_ref,
    x, cot, wg, wu, wd, sign, gate, up, tan, op, own, core_out, core_in, x_out, x_in, cnt_out, cnt_in,
    local_sem, ag_send, ag_recv, core_send, core_recv, x_send, x_recv, cnt_send, cnt_recv,
):
    dp = lax.axis_index("dp")
    me = lax.axis_index("tensor")
    core = lax.rem(dp, 2)
    xi = lax.div(dp, 2)
    yi = lax.div(me, NZ)
    zi = lax.rem(me, NZ)

    away = 1 - 2 * core

    def at_y(step):
        return dp, lax.rem(yi + away * step + NY, NY) * NZ + zi

    def at_z(step):
        return dp, yi * NZ + lax.rem(zi + away * step + NZ, NZ)

    def at_x(step):
        return lax.rem(xi + step + NX, NX) * 2 + core, me

    partner = (xi * 2 + 1 - core, me)

    tok_copy = pltpu.make_async_copy(tok_ref, x.at[pl.ds(0, ROWS), pl.ds(0, D)], local_sem.at[0])
    cot_copy = pltpu.make_async_copy(cot_ref, cot, local_sem.at[1])
    wg_copy = pltpu.make_async_copy(wg_hbm, wg, local_sem.at[2])
    wu_copy = pltpu.make_async_copy(wu_hbm, wu, local_sem.at[3])
    wd_copy = pltpu.make_async_copy(wd_hbm, wd, local_sem.at[4])
    tok_copy.start()
    cot_copy.start()

    peers = [at_y(1), at_y(-1), at_z(1), at_z(-1), partner, at_x(1), at_x(-1), at_x(2)]
    barrier = pltpu.get_barrier_semaphore()
    for peer in peers:
        pl.semaphore_signal(barrier, inc=1, device_id=peer, device_id_type=MESH)

    tok_copy.wait()
    pl.semaphore_wait(barrier, len(peers))

    def block(at, fam):
        start, size = FAM[fam]
        return x.at[pl.ds(at * ROWS, ROWS), pl.ds(start, size)]

    def hop(dy, dz, fam):
        if dy != 0 and (fam == 1 or dz == 0):
            came_dy, came_dz, device = (0, dz, at_y(-dy)) if dy != 2 else (-1, dz, at_y(1))
        else:
            came_dy, came_dz, device = (dy, dz - 1, at_z(-1)) if 0 < dz < 4 else (dy, (dz + 1 if dz < 0 else -3), at_z(1))
        dst = slot(dy, dz)
        return pltpu.make_async_remote_copy(
            src_ref=block(slot(came_dy, came_dz), fam),
            dst_ref=block(dst, fam),
            send_sem=ag_send.at[fam, dst],
            recv_sem=ag_recv.at[fam, dst],
            device_id=device,
            device_id_type=MESH,
        )

    for dst in ((-1, 0, 0), (1, 0, 0), (0, -1, 0), (0, 1, 0)):
        hop(*dst).start()
    row = lax.broadcasted_iota(jnp.int32, (ROWS, 128), 0)
    live = jnp.zeros((ROWS, 128), F32)
    for r in range(ROWS):
        live = jnp.where(row == r, mask_ref[r].astype(F32), live)
    x[0:ROWS, MASK_AT:WIDE] = live.astype(BF16)
    cot_copy.wait()
    x[0:ROWS, D:MASK_AT] = (cot[...].astype(F32) * live[:, 0:1]).astype(BF16)
    for dst in ((0, -1, 1), (0, 1, 1), (-1, 0, 1), (1, 0, 1)):
        hop(*dst).start()

    wg_copy.start()
    wu_copy.start()
    wd_copy.start()
    first_col = me * WIDTH
    col_term = (lax.broadcasted_iota(jnp.int32, (WIDTH, 1), 0) + first_col) * jnp.int32(-1640531535)
    col_term = col_term + seed_ref[0] * jnp.int32(668265263)

    def make_signs(k):
        def run():
            size = D // 8
            i = lax.broadcasted_iota(jnp.int32, (1, size), 1) + k * size
            h = (i * FF) * jnp.int32(-1640531535) + col_term
            h = h ^ lax.shift_right_logical(h, jnp.full_like(h, 15))
            h = h * jnp.int32(739982445)
            h = h ^ lax.shift_right_logical(h, jnp.full_like(h, 12))
            h = h * jnp.int32(695872825)
            h = h ^ lax.shift_left(h, jnp.full_like(h, 15))
            sign[:, k * size : (k + 1) * size] = jnp.where(h < 0, F32(-1.0), F32(1.0)).astype(BF16)

        return run

    def tokens_of(c):
        return slice(c * CHUNK, (c + 1) * CHUNK)

    def make_dot(c, out, w, copy, cols):
        def run():
            if copy is not None:
                copy.wait()
            part = lax.dot_general(w[:, cols], x[tokens_of(c), cols], NT, preferred_element_type=F32)
            if cols.start == 0:
                out[...] = part
            else:
                out[...] += part

        return run

    def make_op(c):
        def run():
            if c == 0:
                wd_copy.wait()
            back = lax.dot_general(wd[...], x[tokens_of(c), D:MASK_AT], NT, preferred_element_type=F32)
            operand = back * up[...] * curvature(gate[...]) * tan[...]
            op[:, tokens_of(c)] = operand.astype(BF16)

        return run

    work = [make_signs(k) for k in range(8)]
    for c in range(N_CHUNK):
        for cols in (slice(0, SPLIT), slice(SPLIT, D)):
            work.append(make_dot(c, gate, wg, wg_copy if c == cols.start == 0 else None, cols))
            work.append(make_dot(c, up, wu, wu_copy if c == cols.start == 0 else None, cols))
            work.append(make_dot(c, tan, sign, None, cols))
        work.append(make_op(c))
    for what, dy, dz, fam in PLAN:
        if what == 0:
            hop(dy, dz, fam).wait_recv()
        elif what == 1:
            hop(dy, dz, fam).start()
        else:
            work[dy]()

    def core_copy(k, part=None):
        rows = pl.ds(0, WIDTH) if part is None else rows_of(part)
        sem = k if part is None else 4 + part
        return pltpu.make_async_remote_copy(
            src_ref=core_out.at[k, rows],
            dst_ref=core_in.at[k, rows],
            send_sem=core_send.at[sem],
            recv_sem=core_recv.at[sem],
            device_id=partner,
            device_id_type=MESH,
        )

    def rows_of(half):
        return pl.ds(half * HALF, HALF)

    def x_copy(k, half, dst, device):
        return pltpu.make_async_remote_copy(
            src_ref=x_out.at[k - 1, rows_of(half)],
            dst_ref=x_in.at[dst, rows_of(half)],
            send_sem=x_send.at[k - 1, half],
            recv_sem=x_recv.at[dst, half],
            device_id=device,
            device_id_type=MESH,
        )

    def product(k, of_core, rows=slice(0, WIDTH)):
        start = (lax.rem(xi + k, NX) * 2 + of_core) * OUT_ROWS
        cols = pl.ds(pl.multiple_of(start, OUT_ROWS), OUT_ROWS)
        return jnp.dot(op[rows, :], x[:, cols], preferred_element_type=F32)

    halves = (slice(0, HALF), slice(HALF, WIDTH))
    for part in (0, 1):
        core_out[2, halves[part]] = product(2, 1 - core, halves[part]).astype(BF16)
        core_copy(2, part).start()
    own[2] = product(2, core)
    core_out[1] = product(1, 1 - core).astype(BF16)
    core_copy(1).start()
    for part, device in ((0, at_x(1)), (1, at_x(-1))):
        core_copy(2, part).wait_recv()
        x_out[1, halves[part]] = (own[2, halves[part]] + core_in[2, halves[part]].astype(F32)).astype(BF16)
        x_copy(2, part, 1, device).start()
    own[1] = product(1, core)
    core_out[3] = product(3, 1 - core).astype(BF16)
    core_copy(3).start()
    core_copy(1).wait_recv()
    own[1] += core_in[1].astype(F32)
    x_out[0, HALF:WIDTH] = own[1, HALF:WIDTH].astype(BF16)
    x_copy(1, 1, 0, at_x(1)).start()
    own[3] = product(3, core)
    core_out[0] = product(0, 1 - core).astype(BF16)
    core_copy(0).start()
    core_copy(3).wait_recv()
    own[3] += core_in[3].astype(F32)
    x_out[2, 0:HALF] = own[3, 0:HALF].astype(BF16)
    x_copy(3, 0, 2, at_x(-1)).start()
    own[0] = product(0, core)

    count = jnp.sum(x[:, MASK_AT:WIDE].astype(F32), axis=0, keepdims=True)
    cnt_out[0] = jnp.broadcast_to(count, (8, 128))

    def count_copy(src, dst, device):
        return pltpu.make_async_remote_copy(
            src_ref=cnt_out.at[src],
            dst_ref=cnt_in.at[dst],
            send_sem=cnt_send.at[dst],
            recv_sem=cnt_recv.at[dst],
            device_id=device,
            device_id_type=MESH,
        )

    count_copy(0, 0, partner).start()

    count_copy(0, 0, partner).wait_recv()
    pair = cnt_out[0] + cnt_in[0]
    cnt_out[1] = pair
    count_copy(1, 1, at_x(1)).start()
    count_copy(1, 2, at_x(2)).start()
    count_copy(1, 3, at_x(-1)).start()
    core_copy(0).wait_recv()
    own[0] += core_in[0].astype(F32)

    x_copy(2, 0, 1, at_x(1)).wait_recv()
    x_out[0, 0:HALF] = (own[1, 0:HALF] + x_in[1, 0:HALF].astype(F32)).astype(BF16)
    x_copy(1, 0, 0, at_x(1)).start()
    x_copy(2, 1, 1, at_x(-1)).wait_recv()
    x_out[2, HALF:WIDTH] = (own[3, HALF:WIDTH] + x_in[1, HALF:WIDTH].astype(F32)).astype(BF16)
    x_copy(3, 1, 2, at_x(-1)).start()

    for d in (1, 2, 3):
        count_copy(1, d, at_x(1)).wait_recv()
    total = pair + cnt_in[1] + cnt_in[2] + cnt_in[3]
    live_count = total[0:1, 0:1]
    own_cols = pl.ds(pl.multiple_of(dp * OUT_ROWS, OUT_ROWS), OUT_ROWS)
    x_copy(1, 1, 0, at_x(1)).wait_recv()
    own[0, HALF:WIDTH] += x_in[0, HALF:WIDTH].astype(F32)
    x_copy(3, 0, 2, at_x(-1)).wait_recv()
    own[0, 0:HALF] += x_in[2, 0:HALF].astype(F32)
    x_copy(1, 0, 0, at_x(1)).wait_recv()
    hess = own[0, 0:HALF] + x_in[0, 0:HALF].astype(F32)
    out_ref[0:HALF, :] = sign[0:HALF, own_cols].astype(F32) * (hess / live_count)
    x_copy(3, 1, 2, at_x(-1)).wait_recv()
    hess = own[0, HALF:WIDTH] + x_in[2, HALF:WIDTH].astype(F32)
    out_ref[HALF:WIDTH, :] = sign[HALF:WIDTH, own_cols].astype(F32) * (hess / live_count)

    for at in range(1, NY * NZ):
        for fam in (0, 1):
            hop(DY[at % 4], DZ[at // 4], fam).wait_send()
    for k in (0, 1, 3):
        core_copy(k).wait_send()
    for part in (0, 1):
        core_copy(2, part).wait_send()
    for k in (1, 2, 3):
        for half in (0, 1):
            x_copy(k, half, 0, at_x(1)).wait_send()
    for d in range(4):
        count_copy(0, d, at_x(1)).wait_send()


def per_device(tokens, cotangent, loss_mask, gate_weight, up_weight, down_weight, probe_seed):
    any_space = pl.BlockSpec(memory_space=pl.ANY)
    smem = pl.BlockSpec(memory_space=pltpu.SMEM)
    vmem = pltpu.VMEM
    dma = pltpu.SemaphoreType.DMA
    out = pl.pallas_call(
        kernel,
        out_shape=jax.ShapeDtypeStruct((WIDTH, OUT_ROWS), F32),
        in_specs=[any_space, any_space, smem, smem, any_space, any_space, any_space],
        out_specs=pl.BlockSpec(memory_space=vmem),
        scratch_shapes=[
            vmem((NY * NZ * ROWS, WIDE), BF16),
            vmem((ROWS, D), BF16),
            vmem((WIDTH, D), BF16),
            vmem((WIDTH, D), BF16),
            vmem((WIDTH, D), BF16),
            vmem((WIDTH, D), BF16),
            vmem((WIDTH, CHUNK), F32),
            vmem((WIDTH, CHUNK), F32),
            vmem((WIDTH, CHUNK), F32),
            vmem((WIDTH, N_CHUNK * CHUNK), BF16),
            vmem((4, WIDTH, OUT_ROWS), F32),
            vmem((4, WIDTH, OUT_ROWS), BF16),
            vmem((4, WIDTH, OUT_ROWS), BF16),
            vmem((3, WIDTH, OUT_ROWS), BF16),
            vmem((3, WIDTH, OUT_ROWS), BF16),
            vmem((2, 8, 128), F32),
            vmem((4, 8, 128), F32),
            dma((5,)),
            dma((2, NY * NZ)),
            dma((2, NY * NZ)),
            dma((6,)),
            dma((6,)),
            dma((3, 2)),
            dma((3, 2)),
            dma((4,)),
            dma((4,)),
        ],
        compiler_params=pltpu.CompilerParams(
            collective_id=0, has_side_effects=True, vmem_limit_bytes=56 * 2**20
        ),
        cost_estimate=pl.CostEstimate(flops=9_400_000_000, bytes_accessed=12_000_000, transcendentals=230_000),
    )(tokens, cotangent, loss_mask, probe_seed, gate_weight.T, up_weight.T, down_weight)
    return out.T


def solution(mesh):
    in_specs = (
        P(("dp", "tensor"), None),
        P(("dp", "tensor"), None),
        P(("dp", "tensor")),
        P(None, "tensor"),
        P(None, "tensor"),
        P("tensor", None),
        P(),
    )
    return jax.shard_map(
        per_device, mesh=mesh, in_specs=in_specs, out_specs=P("dp", "tensor"), check_vma=False
    )
```

```python
import jax
import jax.numpy as jnp
from jax import lax
from jax.experimental import pallas as pl
from jax.experimental.pallas import tpu as pltpu
from jax.sharding import PartitionSpec as P

FF = 14336
D = 4096
NY, NZ, NX = 4, 8, 4
ROWS = 16
WIDTH = 448
CHUNK = 256
N_CHUNK = 2
OUT_ROWS = 512
HALF = WIDTH // 2
MASK_AT = 2 * D
WIDE = 2 * D + 128
SPLIT = 25 * 128
FAM = ((0, SPLIT), (SPLIT, WIDE - SPLIT))
DZ = (0, 1, -1, 2, -2, 3, -3, 4)
DY = (0, 1, -1, 2)
MESH = pl.DeviceIdType.MESH
NT = (((1,), (1,)), ((), ()))
F32 = jnp.float32
BF16 = jnp.bfloat16


def slot(dy, dz):
    return DZ.index(dz) * 4 + DY.index(dy)


PLAN = (
    (2, 0, 0, 0), (2, 1, 0, 0), (2, 2, 0, 0), (2, 3, 0, 0), (2, 4, 0, 0), (2, 5, 0, 0), (2, 6, 0, 0),
    (2, 7, 0, 0), (0, -1, 0, 0), (1, 2, 0, 0), (1, -1, -1, 0), (0, 0, -1, 1), (1, 0, -2, 1), (1, -1, -1, 1),
    (1, 1, -1, 1), (1, -1, 1, 0), (0, 1, 0, 0), (1, 1, -1, 0), (0, 0, 1, 1), (1, 0, 2, 1), (1, -1, 1, 1),
    (1, 1, 1, 1), (1, 1, 1, 0), (0, 2, 0, 0), (1, 2, -1, 0), (0, -1, 0, 1), (1, 2, 0, 1), (1, 2, 1, 0),
    (0, 0, -2, 1), (1, 0, -3, 1), (1, -1, -2, 1), (0, 0, 2, 1), (1, 0, 3, 1), (1, 1, -2, 1), (0, 0, -1, 0),
    (1, 0, -2, 0), (1, -1, 2, 1), (0, 0, 1, 0), (1, 0, 2, 0), (1, 1, 2, 1), (0, -1, -1, 0), (1, -1, -2, 0),
    (0, -1, 1, 0), (1, -1, 2, 0), (0, -1, -1, 1), (1, 2, -1, 1), (0, 1, -1, 0), (1, 1, -2, 0), (0, 1, 1, 0),
    (1, 1, 2, 0), (0, -1, 1, 1), (1, 2, 1, 1), (0, 2, -1, 0), (1, 2, -2, 0), (0, 0, -3, 1), (1, -1, -3, 1),
    (0, 2, 1, 0), (1, 2, 2, 0), (1, 0, 4, 1), (1, 1, -3, 1), (0, 0, -2, 0), (1, 0, -3, 0), (0, 0, 3, 1),
    (1, -1, 3, 1), (0, 0, 2, 0), (1, 0, 3, 0), (0, -1, -2, 0), (1, -1, -3, 0), (1, 1, 3, 1), (0, -1, 2, 0),
    (1, -1, 3, 0), (0, -1, -2, 1), (1, 2, -2, 1), (0, 1, -2, 0), (1, 1, -3, 0), (0, 1, 2, 0), (1, 1, 3, 0),
    (0, -1, 2, 1), (1, 2, 2, 1), (0, 2, -2, 0), (1, 2, -3, 0), (0, 2, 2, 0), (2, 8, 0, 0), (0, 0, 4, 1),
    (1, -1, 4, 1), (1, 2, 3, 0), (2, 9, 0, 0), (0, 0, -3, 0), (1, 0, 4, 0), (2, 10, 0, 0), (1, 1, 4, 1),
    (0, -1, -3, 0), (1, -1, 4, 0), (0, -1, -3, 1), (1, 2, -3, 1), (0, 1, -3, 0), (1, 1, 4, 0), (0, -1, 3, 1),
    (1, 2, 3, 1), (0, 2, -3, 0), (1, 2, 4, 0), (0, 1, 0, 1), (0, 1, -1, 1), (0, 1, 1, 1), (0, 2, 0, 1),
    (0, 1, 2, 1), (0, 2, -1, 1), (0, 2, 1, 1), (0, 2, 2, 1), (2, 11, 0, 0), (2, 12, 0, 0), (2, 13, 0, 0),
    (0, -1, 4, 1), (1, 2, 4, 1), (2, 14, 0, 0), (0, 0, 3, 0), (0, -1, 3, 0), (0, 1, 3, 0), (0, 2, 3, 0),
    (0, 0, 4, 0), (0, -1, 4, 0), (0, 1, 4, 0), (0, 2, 4, 0), (2, 15, 0, 0), (2, 16, 0, 0), (2, 17, 0, 0),
    (0, 1, -2, 1), (0, 1, -3, 1), (0, 1, 3, 1), (0, 2, -2, 1), (0, 1, 4, 1), (0, 2, -3, 1), (0, 2, 3, 1),
    (0, 2, 4, 1), (2, 18, 0, 0), (2, 19, 0, 0), (2, 20, 0, 0), (2, 21, 0, 0),
)


def curvature(gate_pre):
    sigmoid_val = jax.nn.sigmoid(gate_pre)
    return sigmoid_val * (1.0 - sigmoid_val) * (2.0 + gate_pre * (1.0 - 2.0 * sigmoid_val))


def kernel(
    tok_ref, cot_ref, mask_hbm, seed_hbm, wg_hbm, wu_hbm, wd_hbm, out_ref,
    mask_ref, seed_ref, x, cot, wg, wu, wd, sign, gate, up, tan, op, own, core_out, core_in, x_out, x_in, cnt_out, cnt_in,
    local_sem, ag_send, ag_recv, core_send, core_recv, x_send, x_recv, cnt_send, cnt_recv,
):
    dp = lax.axis_index("dp")
    me = lax.axis_index("tensor")
    core = lax.rem(dp, 2)
    xi = lax.div(dp, 2)
    yi = lax.div(me, NZ)
    zi = lax.rem(me, NZ)

    away = 1 - 2 * core

    def at_y(step):
        return dp, lax.rem(yi + away * step + NY, NY) * NZ + zi

    def at_z(step):
        return dp, yi * NZ + lax.rem(zi + away * step + NZ, NZ)

    def at_x(step):
        return lax.rem(xi + step + NX, NX) * 2 + core, me

    partner = (xi * 2 + 1 - core, me)

    tok_copy = pltpu.make_async_copy(tok_ref, x.at[pl.ds(0, ROWS), pl.ds(0, D)], local_sem.at[0])
    cot_copy = pltpu.make_async_copy(cot_ref, cot, local_sem.at[1])
    wg_copy = pltpu.make_async_copy(wg_hbm, wg, local_sem.at[2])
    wu_copy = pltpu.make_async_copy(wu_hbm, wu, local_sem.at[3])
    wd_copy = pltpu.make_async_copy(wd_hbm, wd, local_sem.at[4])
    mask_copy = pltpu.make_async_copy(mask_hbm, mask_ref, local_sem.at[5])
    seed_copy = pltpu.make_async_copy(seed_hbm, seed_ref, local_sem.at[6])
    tok_copy.start()
    cot_copy.start()
    mask_copy.start()
    seed_copy.start()

    peers = [at_y(1), at_y(-1), at_z(1), at_z(-1), partner, at_x(1), at_x(-1), at_x(2)]
    barrier = pltpu.get_barrier_semaphore()
    for peer in peers:
        pl.semaphore_signal(barrier, inc=1, device_id=peer, device_id_type=MESH)

    tok_copy.wait()
    pl.semaphore_wait(barrier, len(peers))

    def block(at, fam):
        start, size = FAM[fam]
        return x.at[pl.ds(at * ROWS, ROWS), pl.ds(start, size)]

    def hop(dy, dz, fam):
        if dy != 0 and (fam == 1 or dz == 0):
            came_dy, came_dz, device = (0, dz, at_y(-dy)) if dy != 2 else (-1, dz, at_y(1))
        else:
            came_dy, came_dz, device = (dy, dz - 1, at_z(-1)) if 0 < dz < 4 else (dy, (dz + 1 if dz < 0 else -3), at_z(1))
        dst = slot(dy, dz)
        return pltpu.make_async_remote_copy(
            src_ref=block(slot(came_dy, came_dz), fam),
            dst_ref=block(dst, fam),
            send_sem=ag_send.at[fam, dst],
            recv_sem=ag_recv.at[fam, dst],
            device_id=device,
            device_id_type=MESH,
        )

    for dst in ((-1, 0, 0), (1, 0, 0), (0, -1, 0), (0, 1, 0)):
        hop(*dst).start()
    row = lax.broadcasted_iota(jnp.int32, (ROWS, 128), 0)
    live = jnp.zeros((ROWS, 128), F32)
    mask_copy.wait()
    for r in range(ROWS):
        live = jnp.where(row == r, mask_ref[r].astype(F32), live)
    x[0:ROWS, MASK_AT:WIDE] = live.astype(BF16)
    cot_copy.wait()
    x[0:ROWS, D:MASK_AT] = (cot[...].astype(F32) * live[:, 0:1]).astype(BF16)
    for dst in ((0, -1, 1), (0, 1, 1), (-1, 0, 1), (1, 0, 1)):
        hop(*dst).start()

    wg_copy.start()
    wu_copy.start()
    wd_copy.start()
    seed_copy.wait()
    first_col = me * WIDTH
    col_term = (lax.broadcasted_iota(jnp.int32, (WIDTH, 1), 0) + first_col) * jnp.int32(-1640531535)
    col_term = col_term + seed_ref[0] * jnp.int32(668265263)

    def make_signs(k):
        def run():
            size = D // 8
            i = lax.broadcasted_iota(jnp.int32, (1, size), 1) + k * size
            h = (i * FF) * jnp.int32(-1640531535) + col_term
            h = h ^ lax.shift_right_logical(h, jnp.full_like(h, 15))
            h = h * jnp.int32(739982445)
            h = h ^ lax.shift_right_logical(h, jnp.full_like(h, 12))
            h = h * jnp.int32(695872825)
            h = h ^ lax.shift_left(h, jnp.full_like(h, 15))
            sign[:, k * size : (k + 1) * size] = jnp.where(h < 0, F32(-1.0), F32(1.0)).astype(BF16)

        return run

    def tokens_of(c):
        return slice(c * CHUNK, (c + 1) * CHUNK)

    def make_dot(c, out, w, copy, cols):
        def run():
            if copy is not None:
                copy.wait()
            part = lax.dot_general(w[:, cols], x[tokens_of(c), cols], NT, preferred_element_type=F32)
            if cols.start == 0:
                out[...] = part
            else:
                out[...] += part

        return run

    def make_op(c):
        def run():
            if c == 0:
                wd_copy.wait()
            back = lax.dot_general(wd[...], x[tokens_of(c), D:MASK_AT], NT, preferred_element_type=F32)
            operand = back * up[...] * curvature(gate[...]) * tan[...]
            op[:, tokens_of(c)] = operand.astype(BF16)

        return run

    work = [make_signs(k) for k in range(8)]
    for c in range(N_CHUNK):
        for cols in (slice(0, SPLIT), slice(SPLIT, D)):
            work.append(make_dot(c, gate, wg, wg_copy if c == cols.start == 0 else None, cols))
            work.append(make_dot(c, up, wu, wu_copy if c == cols.start == 0 else None, cols))
            work.append(make_dot(c, tan, sign, None, cols))
        work.append(make_op(c))
    for what, dy, dz, fam in PLAN:
        if what == 0:
            hop(dy, dz, fam).wait_recv()
        elif what == 1:
            hop(dy, dz, fam).start()
        else:
            work[dy]()

    def core_copy(k, part=None):
        rows = pl.ds(0, WIDTH) if part is None else rows_of(part)
        sem = k if part is None else 4 + part
        return pltpu.make_async_remote_copy(
            src_ref=core_out.at[k, rows],
            dst_ref=core_in.at[k, rows],
            send_sem=core_send.at[sem],
            recv_sem=core_recv.at[sem],
            device_id=partner,
            device_id_type=MESH,
        )

    def rows_of(half):
        return pl.ds(half * HALF, HALF)

    def x_copy(k, half, dst, device):
        return pltpu.make_async_remote_copy(
            src_ref=x_out.at[k - 1, rows_of(half)],
            dst_ref=x_in.at[dst, rows_of(half)],
            send_sem=x_send.at[k - 1, half],
            recv_sem=x_recv.at[dst, half],
            device_id=device,
            device_id_type=MESH,
        )

    def product(k, of_core, rows=slice(0, WIDTH)):
        start = (lax.rem(xi + k, NX) * 2 + of_core) * OUT_ROWS
        cols = pl.ds(pl.multiple_of(start, OUT_ROWS), OUT_ROWS)
        return jnp.dot(op[rows, :], x[:, cols], preferred_element_type=F32)

    halves = (slice(0, HALF), slice(HALF, WIDTH))
    for part in (0, 1):
        core_out[2, halves[part]] = product(2, 1 - core, halves[part]).astype(BF16)
        core_copy(2, part).start()
    own[2] = product(2, core)
    core_out[1] = product(1, 1 - core).astype(BF16)
    core_copy(1).start()
    for part, device in ((0, at_x(1)), (1, at_x(-1))):
        core_copy(2, part).wait_recv()
        x_out[1, halves[part]] = (own[2, halves[part]] + core_in[2, halves[part]].astype(F32)).astype(BF16)
        x_copy(2, part, 1, device).start()
    own[1] = product(1, core)
    core_out[3] = product(3, 1 - core).astype(BF16)
    core_copy(3).start()
    core_copy(1).wait_recv()
    own[1] += core_in[1].astype(F32)
    x_out[0, HALF:WIDTH] = own[1, HALF:WIDTH].astype(BF16)
    x_copy(1, 1, 0, at_x(1)).start()
    own[3] = product(3, core)
    core_out[0] = product(0, 1 - core).astype(BF16)
    core_copy(0).start()
    core_copy(3).wait_recv()
    own[3] += core_in[3].astype(F32)
    x_out[2, 0:HALF] = own[3, 0:HALF].astype(BF16)
    x_copy(3, 0, 2, at_x(-1)).start()
    own[0] = product(0, core)

    count = jnp.sum(x[:, MASK_AT:WIDE].astype(F32), axis=0, keepdims=True)
    cnt_out[0] = jnp.broadcast_to(count, (8, 128))

    def count_copy(src, dst, device):
        return pltpu.make_async_remote_copy(
            src_ref=cnt_out.at[src],
            dst_ref=cnt_in.at[dst],
            send_sem=cnt_send.at[dst],
            recv_sem=cnt_recv.at[dst],
            device_id=device,
            device_id_type=MESH,
        )

    count_copy(0, 0, partner).start()

    count_copy(0, 0, partner).wait_recv()
    pair = cnt_out[0] + cnt_in[0]
    cnt_out[1] = pair
    count_copy(1, 1, at_x(1)).start()
    count_copy(1, 2, at_x(2)).start()
    count_copy(1, 3, at_x(-1)).start()
    core_copy(0).wait_recv()
    own[0] += core_in[0].astype(F32)

    x_copy(2, 0, 1, at_x(1)).wait_recv()
    x_out[0, 0:HALF] = (own[1, 0:HALF] + x_in[1, 0:HALF].astype(F32)).astype(BF16)
    x_copy(1, 0, 0, at_x(1)).start()
    x_copy(2, 1, 1, at_x(-1)).wait_recv()
    x_out[2, HALF:WIDTH] = (own[3, HALF:WIDTH] + x_in[1, HALF:WIDTH].astype(F32)).astype(BF16)
    x_copy(3, 1, 2, at_x(-1)).start()

    for d in (1, 2, 3):
        count_copy(1, d, at_x(1)).wait_recv()
    total = pair + cnt_in[1] + cnt_in[2] + cnt_in[3]
    live_count = total[0:1, 0:1]
    own_cols = pl.ds(pl.multiple_of(dp * OUT_ROWS, OUT_ROWS), OUT_ROWS)
    x_copy(1, 1, 0, at_x(1)).wait_recv()
    own[0, HALF:WIDTH] += x_in[0, HALF:WIDTH].astype(F32)
    x_copy(3, 0, 2, at_x(-1)).wait_recv()
    own[0, 0:HALF] += x_in[2, 0:HALF].astype(F32)
    x_copy(1, 0, 0, at_x(1)).wait_recv()
    hess = own[0, 0:HALF] + x_in[0, 0:HALF].astype(F32)
    out_ref[0:HALF, :] = sign[0:HALF, own_cols].astype(F32) * (hess / live_count)
    x_copy(3, 1, 2, at_x(-1)).wait_recv()
    hess = own[0, HALF:WIDTH] + x_in[2, HALF:WIDTH].astype(F32)
    out_ref[HALF:WIDTH, :] = sign[HALF:WIDTH, own_cols].astype(F32) * (hess / live_count)

    for at in range(1, NY * NZ):
        for fam in (0, 1):
            hop(DY[at % 4], DZ[at // 4], fam).wait_send()
    for k in (0, 1, 3):
        core_copy(k).wait_send()
    for part in (0, 1):
        core_copy(2, part).wait_send()
    for k in (1, 2, 3):
        for half in (0, 1):
            x_copy(k, half, 0, at_x(1)).wait_send()
    for d in range(4):
        count_copy(0, d, at_x(1)).wait_send()


def per_device(tokens, cotangent, loss_mask, gate_weight, up_weight, down_weight, probe_seed):
    any_space = pl.BlockSpec(memory_space=pl.ANY)
    vmem = pltpu.VMEM
    dma = pltpu.SemaphoreType.DMA
    out = pl.pallas_call(
        kernel,
        out_shape=jax.ShapeDtypeStruct((WIDTH, OUT_ROWS), F32),
        in_specs=[any_space] * 7,
        out_specs=pl.BlockSpec(memory_space=vmem),
        scratch_shapes=[
            pltpu.SMEM((ROWS,), jnp.int32),
            pltpu.SMEM((1,), jnp.int32),
            vmem((NY * NZ * ROWS, WIDE), BF16),
            vmem((ROWS, D), BF16),
            vmem((WIDTH, D), BF16),
            vmem((WIDTH, D), BF16),
            vmem((WIDTH, D), BF16),
            vmem((WIDTH, D), BF16),
            vmem((WIDTH, CHUNK), F32),
            vmem((WIDTH, CHUNK), F32),
            vmem((WIDTH, CHUNK), F32),
            vmem((WIDTH, N_CHUNK * CHUNK), BF16),
            vmem((4, WIDTH, OUT_ROWS), F32),
            vmem((4, WIDTH, OUT_ROWS), BF16),
            vmem((4, WIDTH, OUT_ROWS), BF16),
            vmem((3, WIDTH, OUT_ROWS), BF16),
            vmem((3, WIDTH, OUT_ROWS), BF16),
            vmem((2, 8, 128), F32),
            vmem((4, 8, 128), F32),
            dma((7,)),
            dma((2, NY * NZ)),
            dma((2, NY * NZ)),
            dma((6,)),
            dma((6,)),
            dma((3, 2)),
            dma((3, 2)),
            dma((4,)),
            dma((4,)),
        ],
        compiler_params=pltpu.CompilerParams(
            collective_id=0, has_side_effects=True, vmem_limit_bytes=56 * 2**20
        ),
        cost_estimate=pl.CostEstimate(flops=9_400_000_000, bytes_accessed=12_000_000, transcendentals=230_000),
    )(tokens, cotangent, loss_mask, probe_seed, gate_weight.T, up_weight.T, down_weight)
    return out.T


def solution(mesh):
    in_specs = (
        P(("dp", "tensor"), None),
        P(("dp", "tensor"), None),
        P(("dp", "tensor")),
        P(None, "tensor"),
        P(None, "tensor"),
        P("tensor", None),
        P(),
    )
    return jax.shard_map(
        per_device, mesh=mesh, in_specs=in_specs, out_specs=P("dp", "tensor"), check_vma=False
    )
```

```python
import jax
import jax.numpy as jnp
from jax import lax
from jax.experimental import pallas as pl
from jax.experimental.pallas import tpu as pltpu
from jax.sharding import PartitionSpec as P

FF = 14336
D = 4096
NY, NZ, NX = 4, 8, 4
ROWS = 16
WIDTH = 448
CHUNK = 256
N_CHUNK = 2
OUT_ROWS = 512
HALF = WIDTH // 2
MASK_AT = 2 * D
WIDE = 2 * D + 128
SPLIT = 25 * 128
FAM = ((0, SPLIT), (SPLIT, WIDE - SPLIT))
DZ = (0, 1, -1, 2, -2, 3, -3, 4)
DY = (0, 1, -1, 2)
MESH = pl.DeviceIdType.MESH
NT = (((1,), (1,)), ((), ()))
F32 = jnp.float32
BF16 = jnp.bfloat16


def slot(dy, dz):
    return DZ.index(dz) * 4 + DY.index(dy)


PLAN = (
    (2, 0, 0, 0), (2, 1, 0, 0), (2, 2, 0, 0), (2, 3, 0, 0), (2, 4, 0, 0), (2, 5, 0, 0), (2, 6, 0, 0),
    (0, -1, 0, 0), (1, 2, 0, 0), (1, -1, -1, 0), (2, 7, 0, 0), (1, -1, 1, 0), (0, 0, -1, 1), (1, 0, -2, 1),
    (1, -1, -1, 1), (1, 1, -1, 1), (0, 1, 0, 0), (1, 1, -1, 0), (1, 1, 1, 0), (0, 0, 1, 1), (1, 0, 2, 1),
    (1, -1, 1, 1), (1, 1, 1, 1), (0, 2, 0, 0), (1, 2, -1, 0), (0, -1, 0, 1), (1, 2, 0, 1), (1, 2, 1, 0),
    (0, 0, -2, 1), (1, 0, -3, 1), (1, -1, -2, 1), (0, 0, 2, 1), (1, 0, 3, 1), (1, 1, -2, 1), (0, 0, -1, 0),
    (1, 0, -2, 0), (1, -1, 2, 1), (0, 0, 1, 0), (1, 0, 2, 0), (1, 1, 2, 1), (0, -1, -1, 0), (1, -1, -2, 0),
    (0, -1, 1, 0), (1, -1, 2, 0), (0, -1, -1, 1), (1, 2, -1, 1), (0, 1, -1, 0), (1, 1, -2, 0), (0, 1, 1, 0),
    (1, 1, 2, 0), (0, -1, 1, 1), (1, 2, 1, 1), (0, 2, -1, 0), (1, 2, -2, 0), (0, 0, -3, 1), (1, -1, -3, 1),
    (0, 2, 1, 0), (1, 2, 2, 0), (1, 0, 4, 1), (1, 1, -3, 1), (0, 0, -2, 0), (1, 0, -3, 0), (0, 0, 3, 1),
    (1, -1, 3, 1), (0, 0, 2, 0), (1, 0, 3, 0), (0, -1, -2, 0), (1, -1, -3, 0), (1, 1, 3, 1), (0, -1, 2, 0),
    (1, -1, 3, 0), (0, -1, -2, 1), (1, 2, -2, 1), (0, 1, -2, 0), (1, 1, -3, 0), (0, 1, 2, 0), (1, 1, 3, 0),
    (0, -1, 2, 1), (1, 2, 2, 1), (0, 2, -2, 0), (1, 2, -3, 0), (0, 2, 2, 0), (1, 2, 3, 0), (0, 0, 4, 1),
    (1, -1, 4, 1), (2, 8, 0, 0), (0, 0, -3, 0), (1, 0, 4, 0), (1, 1, 4, 1), (2, 9, 0, 0), (2, 10, 0, 0),
    (0, -1, -3, 1), (1, 2, -3, 1), (0, -1, -3, 0), (1, -1, 4, 0), (0, -1, 3, 1), (1, 2, 3, 1), (0, 1, -3, 0),
    (1, 1, 4, 0), (0, 2, -3, 0), (1, 2, 4, 0), (0, 1, 0, 1), (0, 1, -1, 1), (0, 1, 1, 1), (0, 2, 0, 1),
    (0, 1, 2, 1), (0, 2, -1, 1), (0, 2, 1, 1), (0, 2, 2, 1), (2, 11, 0, 0), (2, 12, 0, 0), (2, 13, 0, 0),
    (0, -1, 4, 1), (1, 2, 4, 1), (2, 14, 0, 0), (0, 0, 3, 0), (0, -1, 3, 0), (0, 1, 3, 0), (0, 2, 3, 0),
    (0, 0, 4, 0), (0, -1, 4, 0), (0, 1, 4, 0), (0, 2, 4, 0), (2, 15, 0, 0), (2, 16, 0, 0), (2, 17, 0, 0),
    (0, 1, -2, 1), (0, 1, -3, 1), (0, 1, 3, 1), (0, 2, -2, 1), (0, 1, 4, 1), (0, 2, -3, 1), (0, 2, 3, 1),
    (0, 2, 4, 1), (2, 18, 0, 0), (2, 19, 0, 0), (2, 20, 0, 0), (2, 21, 0, 0),
)


def curvature(gate_pre):
    sigmoid_val = jax.nn.sigmoid(gate_pre)
    return sigmoid_val * (1.0 - sigmoid_val) * (2.0 + gate_pre * (1.0 - 2.0 * sigmoid_val))


def kernel(
    tok_ref, cot_ref, mask_hbm, seed_hbm, wg_hbm, wu_hbm, wd_hbm, out_ref,
    mask_ref, seed_ref, x, cot, wg, wu, wd, sign, gate, up, tan, op, own, core_out, core_in, x_out, x_in, cnt_out, cnt_in,
    local_sem, ag_send, ag_recv, core_send, core_recv, x_send, x_recv, cnt_send, cnt_recv,
):
    dp = lax.axis_index("dp")
    me = lax.axis_index("tensor")
    core = lax.rem(dp, 2)
    xi = lax.div(dp, 2)
    yi = lax.div(me, NZ)
    zi = lax.rem(me, NZ)

    away = 1 - 2 * core

    def at_y(step):
        return dp, lax.rem(yi + away * step + NY, NY) * NZ + zi

    def at_z(step):
        return dp, yi * NZ + lax.rem(zi + away * step + NZ, NZ)

    def at_x(step):
        return lax.rem(xi + step + NX, NX) * 2 + core, me

    partner = (xi * 2 + 1 - core, me)

    tok_copy = pltpu.make_async_copy(tok_ref, x.at[pl.ds(0, ROWS), pl.ds(0, D)], local_sem.at[0])
    cot_copy = pltpu.make_async_copy(cot_ref, cot, local_sem.at[1])
    wg_copy = pltpu.make_async_copy(wg_hbm, wg, local_sem.at[2])
    wu_copy = pltpu.make_async_copy(wu_hbm, wu, local_sem.at[3])
    wd_copy = pltpu.make_async_copy(wd_hbm, wd, local_sem.at[4])
    mask_copy = pltpu.make_async_copy(mask_hbm, mask_ref, local_sem.at[5])
    seed_copy = pltpu.make_async_copy(seed_hbm, seed_ref, local_sem.at[6])
    tok_copy.start()
    cot_copy.start()
    mask_copy.start()
    seed_copy.start()

    peers = [at_y(1), at_y(-1), at_z(1), at_z(-1), partner, at_x(1), at_x(-1), at_x(2)]
    barrier = pltpu.get_barrier_semaphore()
    for peer in peers:
        pl.semaphore_signal(barrier, inc=1, device_id=peer, device_id_type=MESH)

    tok_copy.wait()
    pl.semaphore_wait(barrier, len(peers))

    def block(at, fam):
        start, size = FAM[fam]
        return x.at[pl.ds(at * ROWS, ROWS), pl.ds(start, size)]

    def hop(dy, dz, fam):
        if dy != 0 and (fam == 1 or dz == 0):
            came_dy, came_dz, device = (0, dz, at_y(-dy)) if dy != 2 else (-1, dz, at_y(1))
        else:
            came_dy, came_dz, device = (dy, dz - 1, at_z(-1)) if 0 < dz < 4 else (dy, (dz + 1 if dz < 0 else -3), at_z(1))
        dst = slot(dy, dz)
        return pltpu.make_async_remote_copy(
            src_ref=block(slot(came_dy, came_dz), fam),
            dst_ref=block(dst, fam),
            send_sem=ag_send.at[fam, dst],
            recv_sem=ag_recv.at[fam, dst],
            device_id=device,
            device_id_type=MESH,
        )

    for dst in ((-1, 0, 0), (1, 0, 0), (0, -1, 0), (0, 1, 0)):
        hop(*dst).start()
    row = lax.broadcasted_iota(jnp.int32, (ROWS, 128), 0)
    live = jnp.zeros((ROWS, 128), F32)
    mask_copy.wait()
    for r in range(ROWS):
        live = jnp.where(row == r, mask_ref[r].astype(F32), live)
    x[0:ROWS, MASK_AT:WIDE] = live.astype(BF16)
    cot_copy.wait()
    x[0:ROWS, D:MASK_AT] = (cot[...].astype(F32) * live[:, 0:1]).astype(BF16)
    for dst in ((0, -1, 1), (0, 1, 1), (-1, 0, 1), (1, 0, 1)):
        hop(*dst).start()

    wg_copy.start()
    wu_copy.start()
    wd_copy.start()
    seed_copy.wait()
    first_col = me * WIDTH
    col_term = (lax.broadcasted_iota(jnp.int32, (WIDTH, 1), 0) + first_col) * jnp.int32(-1640531535)
    col_term = col_term + seed_ref[0] * jnp.int32(668265263)

    def make_signs(k):
        def run():
            size = D // 8
            i = lax.broadcasted_iota(jnp.int32, (1, size), 1) + k * size
            h = (i * FF) * jnp.int32(-1640531535) + col_term
            h = h ^ lax.shift_right_logical(h, jnp.full_like(h, 15))
            h = h * jnp.int32(739982445)
            h = h ^ lax.shift_right_logical(h, jnp.full_like(h, 12))
            h = h * jnp.int32(695872825)
            h = h ^ lax.shift_left(h, jnp.full_like(h, 15))
            sign[:, k * size : (k + 1) * size] = jnp.where(h < 0, F32(-1.0), F32(1.0)).astype(BF16)

        return run

    def tokens_of(c):
        return slice(c * CHUNK, (c + 1) * CHUNK)

    def make_dot(c, out, w, copy, cols):
        def run():
            if copy is not None:
                copy.wait()
            part = lax.dot_general(w[:, cols], x[tokens_of(c), cols], NT, preferred_element_type=F32)
            if cols.start == 0:
                out[...] = part
            else:
                out[...] += part

        return run

    def make_op(c):
        def run():
            if c == 0:
                wd_copy.wait()
            back = lax.dot_general(wd[...], x[tokens_of(c), D:MASK_AT], NT, preferred_element_type=F32)
            operand = back * up[...] * curvature(gate[...]) * tan[...]
            op[:, tokens_of(c)] = operand.astype(BF16)

        return run

    work = [make_signs(k) for k in range(8)]
    for c in range(N_CHUNK):
        for cols in (slice(0, SPLIT), slice(SPLIT, D)):
            work.append(make_dot(c, gate, wg, wg_copy if c == cols.start == 0 else None, cols))
            work.append(make_dot(c, up, wu, wu_copy if c == cols.start == 0 else None, cols))
            work.append(make_dot(c, tan, sign, None, cols))
        work.append(make_op(c))
    for what, dy, dz, fam in PLAN:
        if what == 0:
            hop(dy, dz, fam).wait_recv()
        elif what == 1:
            hop(dy, dz, fam).start()
        else:
            work[dy]()

    def core_copy(k, part=None):
        rows = pl.ds(0, WIDTH) if part is None else rows_of(part)
        sem = k if part is None else 4 + part
        return pltpu.make_async_remote_copy(
            src_ref=core_out.at[k, rows],
            dst_ref=core_in.at[k, rows],
            send_sem=core_send.at[sem],
            recv_sem=core_recv.at[sem],
            device_id=partner,
            device_id_type=MESH,
        )

    def rows_of(half):
        return pl.ds(half * HALF, HALF)

    def x_copy(k, half, dst, device):
        return pltpu.make_async_remote_copy(
            src_ref=x_out.at[k - 1, rows_of(half)],
            dst_ref=x_in.at[dst, rows_of(half)],
            send_sem=x_send.at[k - 1, half],
            recv_sem=x_recv.at[dst, half],
            device_id=device,
            device_id_type=MESH,
        )

    def product(k, of_core, rows=slice(0, WIDTH)):
        start = (lax.rem(xi + k, NX) * 2 + of_core) * OUT_ROWS
        cols = pl.ds(pl.multiple_of(start, OUT_ROWS), OUT_ROWS)
        return jnp.dot(op[rows, :], x[:, cols], preferred_element_type=F32)

    halves = (slice(0, HALF), slice(HALF, WIDTH))
    for part in (0, 1):
        core_out[2, halves[part]] = product(2, 1 - core, halves[part]).astype(BF16)
        core_copy(2, part).start()
    own[2] = product(2, core)
    core_out[1] = product(1, 1 - core).astype(BF16)
    core_copy(1).start()
    for part, device in ((0, at_x(1)), (1, at_x(-1))):
        core_copy(2, part).wait_recv()
        x_out[1, halves[part]] = (own[2, halves[part]] + core_in[2, halves[part]].astype(F32)).astype(BF16)
        x_copy(2, part, 1, device).start()
    own[1] = product(1, core)
    core_out[3] = product(3, 1 - core).astype(BF16)
    core_copy(3).start()
    core_copy(1).wait_recv()
    own[1] += core_in[1].astype(F32)
    x_out[0, HALF:WIDTH] = own[1, HALF:WIDTH].astype(BF16)
    x_copy(1, 1, 0, at_x(1)).start()
    own[3] = product(3, core)
    core_out[0] = product(0, 1 - core).astype(BF16)
    core_copy(0).start()
    core_copy(3).wait_recv()
    own[3] += core_in[3].astype(F32)
    x_out[2, 0:HALF] = own[3, 0:HALF].astype(BF16)
    x_copy(3, 0, 2, at_x(-1)).start()
    own[0] = product(0, core)

    count = jnp.sum(x[:, MASK_AT:WIDE].astype(F32), axis=0, keepdims=True)
    cnt_out[0] = jnp.broadcast_to(count, (8, 128))

    def count_copy(src, dst, device):
        return pltpu.make_async_remote_copy(
            src_ref=cnt_out.at[src],
            dst_ref=cnt_in.at[dst],
            send_sem=cnt_send.at[dst],
            recv_sem=cnt_recv.at[dst],
            device_id=device,
            device_id_type=MESH,
        )

    count_copy(0, 0, partner).start()

    count_copy(0, 0, partner).wait_recv()
    pair = cnt_out[0] + cnt_in[0]
    cnt_out[1] = pair
    count_copy(1, 1, at_x(1)).start()
    count_copy(1, 2, at_x(2)).start()
    count_copy(1, 3, at_x(-1)).start()
    core_copy(0).wait_recv()
    own[0] += core_in[0].astype(F32)

    x_copy(2, 0, 1, at_x(1)).wait_recv()
    x_out[0, 0:HALF] = (own[1, 0:HALF] + x_in[1, 0:HALF].astype(F32)).astype(BF16)
    x_copy(1, 0, 0, at_x(1)).start()
    x_copy(2, 1, 1, at_x(-1)).wait_recv()
    x_out[2, HALF:WIDTH] = (own[3, HALF:WIDTH] + x_in[1, HALF:WIDTH].astype(F32)).astype(BF16)
    x_copy(3, 1, 2, at_x(-1)).start()

    for d in (1, 2, 3):
        count_copy(1, d, at_x(1)).wait_recv()
    total = pair + cnt_in[1] + cnt_in[2] + cnt_in[3]
    live_count = total[0:1, 0:1]
    own_cols = pl.ds(pl.multiple_of(dp * OUT_ROWS, OUT_ROWS), OUT_ROWS)
    x_copy(1, 1, 0, at_x(1)).wait_recv()
    own[0, HALF:WIDTH] += x_in[0, HALF:WIDTH].astype(F32)
    x_copy(3, 0, 2, at_x(-1)).wait_recv()
    own[0, 0:HALF] += x_in[2, 0:HALF].astype(F32)
    x_copy(1, 0, 0, at_x(1)).wait_recv()
    hess = own[0, 0:HALF] + x_in[0, 0:HALF].astype(F32)
    out_ref[0:HALF, :] = sign[0:HALF, own_cols].astype(F32) * (hess / live_count)
    x_copy(3, 1, 2, at_x(-1)).wait_recv()
    hess = own[0, HALF:WIDTH] + x_in[2, HALF:WIDTH].astype(F32)
    out_ref[HALF:WIDTH, :] = sign[HALF:WIDTH, own_cols].astype(F32) * (hess / live_count)

    for at in range(1, NY * NZ):
        for fam in (0, 1):
            hop(DY[at % 4], DZ[at // 4], fam).wait_send()
    for k in (0, 1, 3):
        core_copy(k).wait_send()
    for part in (0, 1):
        core_copy(2, part).wait_send()
    for k in (1, 2, 3):
        for half in (0, 1):
            x_copy(k, half, 0, at_x(1)).wait_send()
    for d in range(4):
        count_copy(0, d, at_x(1)).wait_send()


def per_device(tokens, cotangent, loss_mask, gate_weight, up_weight, down_weight, probe_seed):
    any_space = pl.BlockSpec(memory_space=pl.ANY)
    vmem = pltpu.VMEM
    dma = pltpu.SemaphoreType.DMA
    out = pl.pallas_call(
        kernel,
        out_shape=jax.ShapeDtypeStruct((WIDTH, OUT_ROWS), F32),
        in_specs=[any_space] * 7,
        out_specs=pl.BlockSpec(memory_space=vmem),
        scratch_shapes=[
            pltpu.SMEM((ROWS,), jnp.int32),
            pltpu.SMEM((1,), jnp.int32),
            vmem((NY * NZ * ROWS, WIDE), BF16),
            vmem((ROWS, D), BF16),
            vmem((WIDTH, D), BF16),
            vmem((WIDTH, D), BF16),
            vmem((WIDTH, D), BF16),
            vmem((WIDTH, D), BF16),
            vmem((WIDTH, CHUNK), F32),
            vmem((WIDTH, CHUNK), F32),
            vmem((WIDTH, CHUNK), F32),
            vmem((WIDTH, N_CHUNK * CHUNK), BF16),
            vmem((4, WIDTH, OUT_ROWS), F32),
            vmem((4, WIDTH, OUT_ROWS), BF16),
            vmem((4, WIDTH, OUT_ROWS), BF16),
            vmem((3, WIDTH, OUT_ROWS), BF16),
            vmem((3, WIDTH, OUT_ROWS), BF16),
            vmem((2, 8, 128), F32),
            vmem((4, 8, 128), F32),
            dma((7,)),
            dma((2, NY * NZ)),
            dma((2, NY * NZ)),
            dma((6,)),
            dma((6,)),
            dma((3, 2)),
            dma((3, 2)),
            dma((4,)),
            dma((4,)),
        ],
        compiler_params=pltpu.CompilerParams(
            collective_id=0, has_side_effects=True, vmem_limit_bytes=56 * 2**20
        ),
        cost_estimate=pl.CostEstimate(flops=9_400_000_000, bytes_accessed=12_000_000, transcendentals=230_000),
    )(tokens, cotangent, loss_mask, probe_seed, gate_weight.T, up_weight.T, down_weight)
    return out.T


def solution(mesh):
    in_specs = (
        P(("dp", "tensor"), None),
        P(("dp", "tensor"), None),
        P(("dp", "tensor")),
        P(None, "tensor"),
        P(None, "tensor"),
        P("tensor", None),
        P(),
    )
    return jax.shard_map(
        per_device, mesh=mesh, in_specs=in_specs, out_specs=P("dp", "tensor"), check_vma=False
    )
```

```python
import jax
import jax.numpy as jnp
from jax import lax
from jax.experimental import pallas as pl
from jax.experimental.pallas import tpu as pltpu
from jax.sharding import PartitionSpec as P

FF = 14336
D = 4096
NY, NZ, NX = 4, 8, 4
ROWS = 16
WIDTH = 448
CHUNK = 256
N_CHUNK = 2
OUT_ROWS = 512
HALF = WIDTH // 2
MASK_AT = 2 * D
WIDE = 2 * D + 128
SPLIT = 26 * 128
FAM = ((0, SPLIT), (SPLIT, WIDE - SPLIT))
DZ = (0, 1, -1, 2, -2, 3, -3, 4)
DY = (0, 1, -1, 2)
MESH = pl.DeviceIdType.MESH
NT = (((1,), (1,)), ((), ()))
F32 = jnp.float32
BF16 = jnp.bfloat16


def slot(dy, dz):
    return DZ.index(dz) * 4 + DY.index(dy)


PLAN = (
    (2, 0, 0, 0), (2, 1, 0, 0), (2, 2, 0, 0), (2, 3, 0, 0), (2, 4, 0, 0), (2, 5, 0, 0), (2, 6, 0, 0),
    (2, 7, 0, 0), (0, -1, 0, 0), (1, 2, 0, 0), (1, -1, -1, 0), (0, 0, -1, 1), (1, 0, -2, 1), (1, -1, -1, 1),
    (1, 1, -1, 1), (1, -1, 1, 0), (0, 1, 0, 0), (1, 1, -1, 0), (0, 0, 1, 1), (1, 0, 2, 1), (1, -1, 1, 1),
    (1, 1, 1, 1), (1, 1, 1, 0), (0, 2, 0, 0), (1, 2, -1, 0), (0, -1, 0, 1), (1, 2, 0, 1), (1, 2, 1, 0),
    (0, 0, -2, 1), (1, -1, -2, 1), (1, 0, -3, 1), (1, 1, -2, 1), (0, 0, 2, 1), (1, 0, 3, 1), (1, -1, 2, 1),
    (0, 0, -1, 0), (1, 0, -2, 0), (0, 0, 1, 0), (1, 0, 2, 0), (1, 1, 2, 1), (0, -1, -1, 0), (1, -1, -2, 0),
    (0, -1, -1, 1), (1, 2, -1, 1), (0, -1, 1, 0), (1, -1, 2, 0), (0, 1, -1, 0), (1, 1, -2, 0), (0, -1, 1, 1),
    (1, 2, 1, 1), (0, 1, 1, 0), (1, 1, 2, 0), (0, 2, -1, 0), (1, 2, -2, 0), (0, 0, -3, 1), (1, -1, -3, 1),
    (0, 2, 1, 0), (1, 2, 2, 0), (1, 1, -3, 1), (1, 0, 4, 1), (0, 0, 3, 1), (1, -1, 3, 1), (0, 0, -2, 0),
    (1, 0, -3, 0), (0, 0, 2, 0), (1, 0, 3, 0), (1, 1, 3, 1), (0, -1, -2, 0), (1, -1, -3, 0), (0, -1, -2, 1),
    (1, 2, -2, 1), (0, -1, 2, 0), (1, -1, 3, 0), (0, 1, -2, 0), (1, 1, -3, 0), (0, -1, 2, 1), (1, 2, 2, 1),
    (0, 1, 2, 0), (1, 1, 3, 0), (0, 2, -2, 0), (1, 2, -3, 0), (0, 0, 4, 1), (1, -1, 4, 1), (0, 2, 2, 0),
    (2, 8, 0, 0), (1, 2, 3, 0), (1, 1, 4, 1), (2, 9, 0, 0), (0, 0, -3, 0), (1, 0, 4, 0), (2, 10, 0, 0),
    (0, -1, -3, 1), (1, 2, -3, 1), (0, -1, -3, 0), (1, -1, 4, 0), (0, -1, 3, 1), (1, 2, 3, 1), (0, 1, -3, 0),
    (1, 1, 4, 0), (0, 1, 0, 1), (0, 1, -1, 1), (0, 1, 1, 1), (0, 2, 0, 1), (0, 1, 2, 1), (0, 2, -1, 1),
    (0, 2, 1, 1), (0, 2, 2, 1), (2, 11, 0, 0), (2, 12, 0, 0), (2, 13, 0, 0), (0, 2, -3, 0), (1, 2, 4, 0),
    (0, -1, 4, 1), (1, 2, 4, 1), (2, 14, 0, 0), (0, 0, 3, 0), (0, -1, 3, 0), (0, 1, 3, 0), (0, 2, 3, 0),
    (0, 0, 4, 0), (0, -1, 4, 0), (0, 1, 4, 0), (0, 2, 4, 0), (2, 15, 0, 0), (2, 16, 0, 0), (2, 17, 0, 0),
    (0, 1, -2, 1), (0, 1, -3, 1), (0, 1, 3, 1), (0, 2, -2, 1), (0, 1, 4, 1), (0, 2, -3, 1), (0, 2, 3, 1),
    (0, 2, 4, 1), (2, 18, 0, 0), (2, 19, 0, 0), (2, 20, 0, 0), (2, 21, 0, 0),
)


def curvature(gate_pre):
    sigmoid_val = jax.nn.sigmoid(gate_pre)
    return sigmoid_val * (1.0 - sigmoid_val) * (2.0 + gate_pre * (1.0 - 2.0 * sigmoid_val))


def kernel(
    tok_ref, cot_ref, mask_hbm, seed_hbm, wg_hbm, wu_hbm, wd_hbm, out_ref,
    mask_ref, seed_ref, x, cot, wg, wu, wd, sign, gate, up, tan, op, own, core_out, core_in, x_out, x_in, cnt_out, cnt_in,
    local_sem, ag_send, ag_recv, core_send, core_recv, x_send, x_recv, cnt_send, cnt_recv,
):
    dp = lax.axis_index("dp")
    me = lax.axis_index("tensor")
    core = lax.rem(dp, 2)
    xi = lax.div(dp, 2)
    yi = lax.div(me, NZ)
    zi = lax.rem(me, NZ)

    away = 1 - 2 * core

    def at_y(step):
        return dp, lax.rem(yi + away * step + NY, NY) * NZ + zi

    def at_z(step):
        return dp, yi * NZ + lax.rem(zi + away * step + NZ, NZ)

    def at_x(step):
        return lax.rem(xi + step + NX, NX) * 2 + core, me

    partner = (xi * 2 + 1 - core, me)

    tok_copy = pltpu.make_async_copy(tok_ref, x.at[pl.ds(0, ROWS), pl.ds(0, D)], local_sem.at[0])
    cot_copy = pltpu.make_async_copy(cot_ref, cot, local_sem.at[1])
    wg_copy = pltpu.make_async_copy(wg_hbm, wg, local_sem.at[2])
    wu_copy = pltpu.make_async_copy(wu_hbm, wu, local_sem.at[3])
    wd_copy = pltpu.make_async_copy(wd_hbm, wd, local_sem.at[4])
    mask_copy = pltpu.make_async_copy(mask_hbm, mask_ref, local_sem.at[5])
    seed_copy = pltpu.make_async_copy(seed_hbm, seed_ref, local_sem.at[6])
    tok_copy.start()
    cot_copy.start()
    mask_copy.start()
    seed_copy.start()

    peers = [at_y(1), at_y(-1), at_z(1), at_z(-1), partner, at_x(1), at_x(-1), at_x(2)]
    barrier = pltpu.get_barrier_semaphore()
    for peer in peers:
        pl.semaphore_signal(barrier, inc=1, device_id=peer, device_id_type=MESH)

    tok_copy.wait()
    pl.semaphore_wait(barrier, len(peers))

    def block(at, fam):
        start, size = FAM[fam]
        return x.at[pl.ds(at * ROWS, ROWS), pl.ds(start, size)]

    def hop(dy, dz, fam):
        if dy != 0 and (fam == 1 or dz == 0):
            came_dy, came_dz, device = (0, dz, at_y(-dy)) if dy != 2 else (-1, dz, at_y(1))
        else:
            came_dy, came_dz, device = (dy, dz - 1, at_z(-1)) if 0 < dz < 4 else (dy, (dz + 1 if dz < 0 else -3), at_z(1))
        dst = slot(dy, dz)
        return pltpu.make_async_remote_copy(
            src_ref=block(slot(came_dy, came_dz), fam),
            dst_ref=block(dst, fam),
            send_sem=ag_send.at[fam, dst],
            recv_sem=ag_recv.at[fam, dst],
            device_id=device,
            device_id_type=MESH,
        )

    for dst in ((-1, 0, 0), (1, 0, 0), (0, -1, 0), (0, 1, 0)):
        hop(*dst).start()
    row = lax.broadcasted_iota(jnp.int32, (ROWS, 128), 0)
    live = jnp.zeros((ROWS, 128), F32)
    mask_copy.wait()
    for r in range(ROWS):
        live = jnp.where(row == r, mask_ref[r].astype(F32), live)
    x[0:ROWS, MASK_AT:WIDE] = live.astype(BF16)
    cot_copy.wait()
    x[0:ROWS, D:MASK_AT] = (cot[...].astype(F32) * live[:, 0:1]).astype(BF16)
    for dst in ((0, -1, 1), (0, 1, 1), (-1, 0, 1), (1, 0, 1)):
        hop(*dst).start()

    wg_copy.start()
    wu_copy.start()
    wd_copy.start()
    seed_copy.wait()
    first_col = me * WIDTH
    col_term = (lax.broadcasted_iota(jnp.int32, (WIDTH, 1), 0) + first_col) * jnp.int32(-1640531535)
    col_term = col_term + seed_ref[0] * jnp.int32(668265263)

    def make_signs(k):
        def run():
            size = D // 8
            i = lax.broadcasted_iota(jnp.int32, (1, size), 1) + k * size
            h = (i * FF) * jnp.int32(-1640531535) + col_term
            h = h ^ lax.shift_right_logical(h, jnp.full_like(h, 15))
            h = h * jnp.int32(739982445)
            h = h ^ lax.shift_right_logical(h, jnp.full_like(h, 12))
            h = h * jnp.int32(695872825)
            h = h ^ lax.shift_left(h, jnp.full_like(h, 15))
            sign[:, k * size : (k + 1) * size] = jnp.where(h < 0, F32(-1.0), F32(1.0)).astype(BF16)

        return run

    def tokens_of(c):
        return slice(c * CHUNK, (c + 1) * CHUNK)

    def make_dot(c, out, w, copy, cols):
        def run():
            if copy is not None:
                copy.wait()
            part = lax.dot_general(w[:, cols], x[tokens_of(c), cols], NT, preferred_element_type=F32)
            if cols.start == 0:
                out[...] = part
            else:
                out[...] += part

        return run

    def make_op(c):
        def run():
            if c == 0:
                wd_copy.wait()
            back = lax.dot_general(wd[...], x[tokens_of(c), D:MASK_AT], NT, preferred_element_type=F32)
            operand = back * up[...] * curvature(gate[...]) * tan[...]
            op[:, tokens_of(c)] = operand.astype(BF16)

        return run

    work = [make_signs(k) for k in range(8)]
    for c in range(N_CHUNK):
        for cols in (slice(0, SPLIT), slice(SPLIT, D)):
            work.append(make_dot(c, gate, wg, wg_copy if c == cols.start == 0 else None, cols))
            work.append(make_dot(c, up, wu, wu_copy if c == cols.start == 0 else None, cols))
            work.append(make_dot(c, tan, sign, None, cols))
        work.append(make_op(c))
    for what, dy, dz, fam in PLAN:
        if what == 0:
            hop(dy, dz, fam).wait_recv()
        elif what == 1:
            hop(dy, dz, fam).start()
        else:
            work[dy]()

    def core_copy(k, part=None):
        rows = pl.ds(0, WIDTH) if part is None else rows_of(part)
        sem = k if part is None else 4 + part
        return pltpu.make_async_remote_copy(
            src_ref=core_out.at[k, rows],
            dst_ref=core_in.at[k, rows],
            send_sem=core_send.at[sem],
            recv_sem=core_recv.at[sem],
            device_id=partner,
            device_id_type=MESH,
        )

    def rows_of(half):
        return pl.ds(half * HALF, HALF)

    def x_copy(k, half, dst, device):
        return pltpu.make_async_remote_copy(
            src_ref=x_out.at[k - 1, rows_of(half)],
            dst_ref=x_in.at[dst, rows_of(half)],
            send_sem=x_send.at[k - 1, half],
            recv_sem=x_recv.at[dst, half],
            device_id=device,
            device_id_type=MESH,
        )

    def product(k, of_core, rows=slice(0, WIDTH)):
        start = (lax.rem(xi + k, NX) * 2 + of_core) * OUT_ROWS
        cols = pl.ds(pl.multiple_of(start, OUT_ROWS), OUT_ROWS)
        return jnp.dot(op[rows, :], x[:, cols], preferred_element_type=F32)

    halves = (slice(0, HALF), slice(HALF, WIDTH))
    for part in (0, 1):
        core_out[2, halves[part]] = product(2, 1 - core, halves[part]).astype(BF16)
        core_copy(2, part).start()
    own[2] = product(2, core)
    core_out[1] = product(1, 1 - core).astype(BF16)
    core_copy(1).start()
    for part, device in ((0, at_x(1)), (1, at_x(-1))):
        core_copy(2, part).wait_recv()
        x_out[1, halves[part]] = (own[2, halves[part]] + core_in[2, halves[part]].astype(F32)).astype(BF16)
        x_copy(2, part, 1, device).start()
    own[1] = product(1, core)
    core_out[3] = product(3, 1 - core).astype(BF16)
    core_copy(3).start()
    core_copy(1).wait_recv()
    own[1] += core_in[1].astype(F32)
    x_out[0, HALF:WIDTH] = own[1, HALF:WIDTH].astype(BF16)
    x_copy(1, 1, 0, at_x(1)).start()
    own[3] = product(3, core)
    core_out[0] = product(0, 1 - core).astype(BF16)
    core_copy(0).start()
    core_copy(3).wait_recv()
    own[3] += core_in[3].astype(F32)
    x_out[2, 0:HALF] = own[3, 0:HALF].astype(BF16)
    x_copy(3, 0, 2, at_x(-1)).start()
    own[0] = product(0, core)

    count = jnp.sum(x[:, MASK_AT:WIDE].astype(F32), axis=0, keepdims=True)
    cnt_out[0] = jnp.broadcast_to(count, (8, 128))

    def count_copy(src, dst, device):
        return pltpu.make_async_remote_copy(
            src_ref=cnt_out.at[src],
            dst_ref=cnt_in.at[dst],
            send_sem=cnt_send.at[dst],
            recv_sem=cnt_recv.at[dst],
            device_id=device,
            device_id_type=MESH,
        )

    count_copy(0, 0, partner).start()

    count_copy(0, 0, partner).wait_recv()
    pair = cnt_out[0] + cnt_in[0]
    cnt_out[1] = pair
    count_copy(1, 1, at_x(1)).start()
    count_copy(1, 2, at_x(2)).start()
    count_copy(1, 3, at_x(-1)).start()
    core_copy(0).wait_recv()
    own[0] += core_in[0].astype(F32)

    x_copy(2, 0, 1, at_x(1)).wait_recv()
    x_out[0, 0:HALF] = (own[1, 0:HALF] + x_in[1, 0:HALF].astype(F32)).astype(BF16)
    x_copy(1, 0, 0, at_x(1)).start()
    x_copy(2, 1, 1, at_x(-1)).wait_recv()
    x_out[2, HALF:WIDTH] = (own[3, HALF:WIDTH] + x_in[1, HALF:WIDTH].astype(F32)).astype(BF16)
    x_copy(3, 1, 2, at_x(-1)).start()

    for d in (1, 2, 3):
        count_copy(1, d, at_x(1)).wait_recv()
    total = pair + cnt_in[1] + cnt_in[2] + cnt_in[3]
    live_count = total[0:1, 0:1]
    own_cols = pl.ds(pl.multiple_of(dp * OUT_ROWS, OUT_ROWS), OUT_ROWS)
    x_copy(1, 1, 0, at_x(1)).wait_recv()
    own[0, HALF:WIDTH] += x_in[0, HALF:WIDTH].astype(F32)
    x_copy(3, 0, 2, at_x(-1)).wait_recv()
    own[0, 0:HALF] += x_in[2, 0:HALF].astype(F32)
    x_copy(1, 0, 0, at_x(1)).wait_recv()
    hess = own[0, 0:HALF] + x_in[0, 0:HALF].astype(F32)
    out_ref[0:HALF, :] = sign[0:HALF, own_cols].astype(F32) * (hess / live_count)
    x_copy(3, 1, 2, at_x(-1)).wait_recv()
    hess = own[0, HALF:WIDTH] + x_in[2, HALF:WIDTH].astype(F32)
    out_ref[HALF:WIDTH, :] = sign[HALF:WIDTH, own_cols].astype(F32) * (hess / live_count)

    for at in range(1, NY * NZ):
        for fam in (0, 1):
            hop(DY[at % 4], DZ[at // 4], fam).wait_send()
    for k in (0, 1, 3):
        core_copy(k).wait_send()
    for part in (0, 1):
        core_copy(2, part).wait_send()
    for k in (1, 2, 3):
        for half in (0, 1):
            x_copy(k, half, 0, at_x(1)).wait_send()
    for d in range(4):
        count_copy(0, d, at_x(1)).wait_send()


def per_device(tokens, cotangent, loss_mask, gate_weight, up_weight, down_weight, probe_seed):
    any_space = pl.BlockSpec(memory_space=pl.ANY)
    vmem = pltpu.VMEM
    dma = pltpu.SemaphoreType.DMA
    out = pl.pallas_call(
        kernel,
        out_shape=jax.ShapeDtypeStruct((WIDTH, OUT_ROWS), F32),
        in_specs=[any_space] * 7,
        out_specs=pl.BlockSpec(memory_space=vmem),
        scratch_shapes=[
            pltpu.SMEM((ROWS,), jnp.int32),
            pltpu.SMEM((1,), jnp.int32),
            vmem((NY * NZ * ROWS, WIDE), BF16),
            vmem((ROWS, D), BF16),
            vmem((WIDTH, D), BF16),
            vmem((WIDTH, D), BF16),
            vmem((WIDTH, D), BF16),
            vmem((WIDTH, D), BF16),
            vmem((WIDTH, CHUNK), F32),
            vmem((WIDTH, CHUNK), F32),
            vmem((WIDTH, CHUNK), F32),
            vmem((WIDTH, N_CHUNK * CHUNK), BF16),
            vmem((4, WIDTH, OUT_ROWS), F32),
            vmem((4, WIDTH, OUT_ROWS), BF16),
            vmem((4, WIDTH, OUT_ROWS), BF16),
            vmem((3, WIDTH, OUT_ROWS), BF16),
            vmem((3, WIDTH, OUT_ROWS), BF16),
            vmem((2, 8, 128), F32),
            vmem((4, 8, 128), F32),
            dma((7,)),
            dma((2, NY * NZ)),
            dma((2, NY * NZ)),
            dma((6,)),
            dma((6,)),
            dma((3, 2)),
            dma((3, 2)),
            dma((4,)),
            dma((4,)),
        ],
        compiler_params=pltpu.CompilerParams(
            collective_id=0, has_side_effects=True, vmem_limit_bytes=56 * 2**20
        ),
        cost_estimate=pl.CostEstimate(flops=9_400_000_000, bytes_accessed=12_000_000, transcendentals=230_000),
    )(tokens, cotangent, loss_mask, probe_seed, gate_weight.T, up_weight.T, down_weight)
    return out.T


def solution(mesh):
    in_specs = (
        P(("dp", "tensor"), None),
        P(("dp", "tensor"), None),
        P(("dp", "tensor")),
        P(None, "tensor"),
        P(None, "tensor"),
        P("tensor", None),
        P(),
    )
    return jax.shard_map(
        per_device, mesh=mesh, in_specs=in_specs, out_specs=P("dp", "tensor"), check_vma=False
    )
```
